256 devices in a mesh: tm: 32 (over x, z), space: 8 (over y, core).
Axes of the slice: x: 4, y: 4, z: 8, core: 2. Of those that a mesh axis runs over, the one named last changes fastest.
Arguments:
- state: float32 [64, 4, 64, 1024], P('tm', None, 'space'), may hold values from -6 to 6
- adjoint: float32 [64, 4, 64, 1024], P('tm', None, 'space'), may hold values from -6 to 6
- source: float32 [64, 4, 64, 1024], P('tm', None, 'space'), may hold values from -6 to 6
- target: float32 [64, 4, 64, 1024], P('tm', None, 'space'), may hold values from -6 to 6
- conductivity: float32 [4, 64, 1024], P(None, 'space'), may hold values from 0.5 to 2
Outputs:
- new_state: float32 [64, 4, 64, 1024], P('tm', None, 'space')
- new_adjoint: float32 [64, 4, 64, 1024], P('tm', None, 'space')
The draws below stay inside these ranges and needn't reach their ends.
All inputs are finite; a program needn't handle non-finite values.
Results may differ from the reference program's by a relative error of at most 0.0003.
Values sent between devices are 32-bit elements; how exact they have to be, the bound alone decides.
No kernel may reach another device: no remote copies, remote signals or barrier semaphores. Data moves between devices by JAX's collectives and lax.ppermute only.
A program may use at most 128 MiB of HBM per device.

```python
import math
import jax
import jax.numpy as jnp
from jax import lax

PLANES = 4
COLS = 1024
SWEEPS = 8
NT = 64
NR = 64


def block_scale(key, shape, shards, smallest, high):
    factor_of, own = 1.0, jax.random.fold_in(key, 6)
    for axis_at, blocks in shards:
        draws = jnp.exp(jax.random.uniform(jax.random.fold_in(own, axis_at), (blocks,), jnp.float32, smallest / len(shards), high / len(shards)))
        factor_of = factor_of * jnp.repeat(draws, shape[axis_at] // blocks).reshape([-1 if axis == axis_at else 1 for axis in range(len(shape))])
    return factor_of


def gaussian(key, dims, scale, reach, shards=(), kind=jnp.bfloat16):
    array = scale * jax.random.normal(key, dims, jnp.float32)
    if shards:
        array = array * block_scale(key, dims, shards, -0.22, 0.18)
    return jnp.clip(array, -reach, reach).astype(kind)


def setup_inputs(seed: int = 0) -> dict:
    key_list = jax.random.split(jax.random.key(seed), 6)
    return {
        "state": gaussian(key_list[0], (NT, PLANES, NR, COLS), 1.0, 6.0, ((0, 32), (2, 8)), jnp.float32),
        "adjoint": gaussian(key_list[1], (NT, PLANES, NR, COLS), 1.0, 6.0, ((0, 32), (2, 8)), jnp.float32),
        "source": gaussian(key_list[2], (NT, PLANES, NR, COLS), 1.0, 6.0, ((0, 32), (2, 8)), jnp.float32),
        "target": gaussian(key_list[3], (NT, PLANES, NR, COLS), 1.0, 6.0, ((0, 32), (2, 8)), jnp.float32),
        "conductivity": jnp.clip(jnp.exp(math.log(2.0) - 1.3862944 * jax.random.uniform(key_list[4], (PLANES, NR, COLS), jnp.float32) ** block_scale(key_list[4], (PLANES, NR, COLS), ((1, 8),), -0.2, 0.2)), 0.5, 2.0),
    }


step_scale = 0.5
penalty = 0.05


def faces(padded):
    return [padded[..., :-2, 1:-1, 1:-1], padded[..., 2:, 1:-1, 1:-1],
            padded[..., 1:-1, :-2, 1:-1], padded[..., 1:-1, 2:, 1:-1],
            padded[..., 1:-1, 1:-1, :-2], padded[..., 1:-1, 1:-1, 2:]]


def pad_space(field):
    widths = [(0, 0)] * (field.ndim - 3) + [(1, 1)] * 3
    return jnp.pad(field, widths)


def neighbours(field, weights):
    total = jnp.zeros(field.shape, jnp.float32)
    for weight, near in zip(weights, faces(pad_space(field))):
        total = total + weight * near
    return total


def apply_inverse(rhs, big_a, big_b, inverse):
    coupling = step_scale / penalty
    ur, vr, ui, vi = rhs[0], rhs[1], rhs[2], rhs[3]
    return jnp.stack([(big_a * ur + big_b * ui - coupling * vr) * inverse,
                      (step_scale * ur + big_a * vr - big_b * vi) * inverse,
                      (big_a * ui - big_b * ur - coupling * vi) * inverse,
                      (step_scale * ui + big_a * vi + big_b * vr) * inverse])


def reference(state, adjoint, source, target, conductivity):
    weights = [0.5 * (conductivity + near) for near in faces(pad_space(conductivity))]
    diag = jnp.zeros(conductivity.shape, jnp.float32)
    for weight in weights:
        diag = diag + weight
    k_state = diag * state - neighbours(state, weights)
    k_adjoint = diag * adjoint - neighbours(adjoint, weights)
    state_prev = jnp.roll(state, 1, axis=0)
    adjoint_next = jnp.roll(adjoint, -1, axis=0)
    h = step_scale
    state_res = h * source - (state - state_prev + h * k_state + (h / penalty) * adjoint)
    adjoint_res = -h * target - (adjoint - adjoint_next + h * k_adjoint - h * state)
    spec_state = jnp.fft.fft(state_res, axis=0)
    spec_adjoint = jnp.fft.fft(adjoint_res, axis=0)
    spectrum = jnp.stack([jnp.real(spec_state), jnp.real(spec_adjoint),
                          jnp.imag(spec_state), jnp.imag(spec_adjoint)], axis=1)
    theta = 2.0 * math.pi * jnp.arange(NT).astype(jnp.float32) / NT

    def solve_one(item):
        rhs, angle = item
        big_a = (1.0 - jnp.cos(angle)) + h * diag
        big_b = jnp.sin(angle)
        inverse = 1.0 / (big_a * big_a + big_b * big_b + h * h / penalty)
        guess = apply_inverse(rhs, big_a, big_b, inverse)
        for sweep in range(SWEEPS - 1):
            guess = apply_inverse(rhs + h * neighbours(guess, weights), big_a, big_b, inverse)
        return guess

    solved = lax.map(solve_one, (spectrum, theta))
    back_state = jnp.real(jnp.fft.ifft(lax.complex(solved[:, 0], solved[:, 2]), axis=0))
    back_adjoint = jnp.real(jnp.fft.ifft(lax.complex(solved[:, 1], solved[:, 3]), axis=0))
    return state + back_state, adjoint + back_adjoint
```

```python
import functools
import math

import jax
import jax.numpy as jnp
import ml_dtypes
import numpy as np
from jax import lax
from jax.experimental import pallas as pl
from jax.experimental.pallas import tpu as pltpu
from jax.sharding import PartitionSpec as P

SWEEPS = 8
STEP = 0.5
PENALTY = 0.05
LANES = 128
WIDE = 8
DEEP = SWEEPS - 1
VMEM_LIMIT = 56 * 1024 * 1024


def transforms(period):
    q = STEP / PENALTY
    time = np.arange(period)
    pairs = [(0, 1)] + [(k, s) for k in range(1, period // 2) for s in (1, -1)] + [(period // 2, 1)]
    count = len(pairs)
    forward = np.zeros((period, 2, 2 * count))
    inverse = np.zeros((2 * count, period, 2))
    real_shift, imag_shift = np.zeros(count), np.zeros(count)
    for m, (k, sign) in enumerate(pairs):
        theta = 2.0 * math.pi * k / period
        sine = 0.0 if k in (0, period // 2) else math.sin(theta)
        root = math.sqrt(sine * sine + STEP * q)
        real_shift[m] = 1.0 - math.cos(theta)
        imag_shift[m] = sign * root
        wave = np.exp(-1j * theta * time)
        first = (root + sign * sine) / (2.0 * q * root) * wave
        second = -sign * 1j / (2.0 * root) * wave
        for f, row in enumerate((first, second)):
            forward[:, f, m] = row.real
            forward[:, f, count + m] = row.imag
        weight = 2.0 / period
        back = np.conj(wave) * weight
        for f, factor in enumerate((q, sign * 1j * (root - sign * sine))):
            inverse[m, :, f] = (factor * back).real
            inverse[count + m, :, f] = -(factor * back).imag
    real_lane = np.concatenate([real_shift, real_shift])
    imag_lane = np.concatenate([imag_shift, -imag_shift])
    return forward, inverse, np.stack([real_lane, imag_lane]).astype(np.float32)


def split_const(matrix):
    high = matrix.astype(np.float32).astype(ml_dtypes.bfloat16)
    low = (matrix - high.astype(np.float64)).astype(np.float32).astype(ml_dtypes.bfloat16)
    return high, low


def dot_split(left, high_ref, low_ref):
    high = left.astype(jnp.bfloat16)
    low = (left - high.astype(jnp.float32)).astype(jnp.bfloat16)
    dot = functools.partial(jnp.dot, preferred_element_type=jnp.float32)
    return dot(high, high_ref[...]) + (dot(low, high_ref[...]) + dot(high, low_ref[...]))


def residual_kernel(blocks, state, adjoint, source, target, prior, later, top, bottom, cond, out, res, turned):
    steps, planes, rows, cols = state.shape
    row = lax.broadcasted_iota(jnp.int32, (rows, cols), 0)
    col = lax.broadcasted_iota(jnp.int32, (rows, cols), 1)

    def near(value, above, below):
        up = jnp.where(row == 0, above, pltpu.roll(value, 1, axis=0))
        down = jnp.where(row == rows - 1, below, pltpu.roll(value, rows - 1, axis=0))
        left = jnp.where(col == 0, 0.0, pltpu.roll(value, 1, axis=1))
        right = jnp.where(col == cols - 1, 0.0, pltpu.roll(value, cols - 1, axis=1))
        return up, down, left, right

    edge = 2 * steps * planes
    kappa = [cond[p] for p in range(planes)]
    zero = jnp.zeros((rows, cols), jnp.float32)
    for p in range(planes):
        around = near(kappa[p], top[pl.ds(edge + p, 1)], bottom[pl.ds(edge + p, 1)])
        around += (kappa[p - 1] if p else zero, kappa[p + 1] if p < planes - 1 else zero)
        weights = [(0.5 * STEP) * (kappa[p] + k) for k in around]
        diag = weights[0]
        for w in weights[1:]:
            diag = diag + w
        for t in range(steps):
            stiff = []
            for f, field in enumerate((state, adjoint)):
                at = (f * steps + t) * planes + p
                value = field[t, p]
                sides = near(value, top[pl.ds(at, 1)], bottom[pl.ds(at, 1)])
                total = diag * value
                for w, v in zip(weights, sides):
                    total = total - w * v
                if p:
                    total = total - weights[4] * field[t, p - 1]
                if p < planes - 1:
                    total = total - weights[5] * field[t, p + 1]
                stiff.append(total)
            s, a = state[t, p], adjoint[t, p]
            before = state[t - 1, p] if t else prior[p]
            after = adjoint[t + 1, p] if t < steps - 1 else later[p]
            first = STEP * source[t, p] - (s - before + stiff[0] + (STEP / PENALTY) * a)
            second = -STEP * target[t, p] - (a - after + stiff[1] - STEP * s)
            for f, value in enumerate((first, second)):
                res[pl.ds(((t * 2 + f) * planes + p) * rows, rows), :] = value
    turned[pl.ds(0, WIDE), :] = jnp.zeros((WIDE, LANES), jnp.float32)
    turned[pl.ds(WIDE + cols, WIDE), :] = jnp.zeros((WIDE, LANES), jnp.float32)
    for tile in range(cols // LANES):
        turned[pl.ds(WIDE + tile * LANES, LANES), :] = res[:, pl.ds(tile * LANES, LANES)].T
    own = cols // blocks
    for j in range(blocks):
        out[j] = turned[pl.ds(j * own, own + 2 * WIDE), :]


def forward_kernel(shape, got, high, low, own, up, down, left):
    blocks, span, planes, rows = shape
    half = span // 2
    cells = planes * rows
    for g in range(span // 4):
        parts = [got[pl.ds(4 * g + c, blocks, stride=span), :] for c in range(4)]
        turned = jnp.concatenate(parts, axis=0).T
        for tf in range(4):
            left[pl.ds(g * cells, cells), pl.ds(tf * LANES, LANES)] = turned[tf * cells : (tf + 1) * cells]
    spectrum = dot_split(left[...], high, low)
    for g in range(span // 4):
        for c in range(4):
            side, at = divmod(4 * g + c, half)
            for p in range(planes):
                piece = spectrum[g * cells + p * rows : g * cells + (p + 1) * rows, c * LANES : (c + 1) * LANES]
                own[pl.ds(at * 2 * planes + side * planes + p, rows, stride=half * 2 * planes), :] = piece
    size = half * 2 * planes * DEEP
    up[...] = own[pl.ds(0, size), :]
    down[...] = own[pl.ds(half * 2 * planes, size), :]


def sweep_kernel(shape, own, above, below, kappa, shifts, high, low, out, rhs, first, second, w_row, w_col, w_plane, w_back, scale, cross, left):
    blocks, half, planes, rows = shape
    tall = rows + 2 * DEEP
    depth = 2 * planes
    block = (half, depth, LANES)

    position = lax.broadcasted_iota(jnp.int32, block, 1) % planes

    def beside(value):
        before = jnp.concatenate([pltpu.roll(value[half - 1], planes, axis=0)[None], value[:-1]], axis=0)
        after = jnp.concatenate([value[1:], pltpu.roll(value[0], planes, axis=0)[None]], axis=0)
        return before, after

    def bond(a, b):
        return jnp.where(a * b > 0.0, (0.5 * STEP) * (a + b), 0.0)

    side = lax.broadcasted_iota(jnp.int32, (half, depth, LANES), 1) // planes
    column = lax.broadcasted_iota(jnp.int32, (half, depth, LANES), 0)
    real = shifts[0:1, :][None]
    imag = shifts[1:2, :][None]

    def setup(r, _):
        k = kappa[r + 1]
        k_up, k_down = kappa[r], kappa[r + 2]
        k_left, k_right = beside(k)
        k_left = jnp.where((column == 0) & (side == 0), 0.0, k_left)
        k_right = jnp.where((column == half - 1) & (side == 1), 0.0, k_right)
        k_back = jnp.where(position == 0, 0.0, pltpu.roll(k, 1, axis=1))
        k_front = jnp.where(position == planes - 1, 0.0, pltpu.roll(k, depth - 1, axis=1))
        w_row[r] = bond(k, k_down)
        w_col[r] = bond(k, k_right)
        w_plane[r] = bond(k, k_front)
        w_back[r] = bond(k, k_back)
        big = (0.5 * STEP) * (6.0 * k + (k_up + k_down + k_left + k_right + k_back + k_front)) + real
        inv = 1.0 / (big * big + imag * imag)
        scale[r] = big * inv
        cross[r] = imag * inv

    lax.fori_loop(0, tall, setup, None)

    rhs[pl.ds(0, DEEP)] = above[...]
    rhs[pl.ds(DEEP, rows)] = own[...]
    rhs[pl.ds(DEEP + rows, DEEP)] = below[...]

    def solve(total, r):
        return scale[r] * total + cross[r] * pltpu.roll(total, LANES // 2, axis=2)

    def start(r, _):
        first[r] = solve(rhs[r], r)

    lax.fori_loop(0, tall, start, None)
    old, new = first, second
    for sweep in range(1, SWEEPS):

        def step(r, _, old=old, new=new):
            value = old[r]
            before, after = beside(value)
            weight = w_col[r]
            weight_before, _ = beside(weight)
            total = rhs[r] + weight * after + weight_before * before
            total = total + w_row[r] * old[r + 1] + w_row[r - 1] * old[r - 1]
            total = total + w_plane[r] * pltpu.roll(value, depth - 1, axis=1)
            total = total + w_back[r] * pltpu.roll(value, 1, axis=1)
            new[r] = solve(total, r)

        lax.fori_loop(sweep, tall - sweep, step, None)
        old, new = new, old

    cells = planes * rows
    own_cols = 2 * half - 2 * WIDE
    for g in range(own_cols // 4):
        for c in range(4):
            side_at, at = divmod(4 * g + c + WIDE, half)
            for p in range(planes):
                piece = old[pl.ds(DEEP, rows), at, side_at * planes + p, :]
                left[pl.ds(g * cells + p * rows, rows), pl.ds(c * LANES, LANES)] = piece
    values = dot_split(left[...], high, low)
    for g in range(own_cols // 4):
        parts = [values[g * cells : (g + 1) * cells, tf * LANES : (tf + 1) * LANES] for tf in range(4)]
        turned = jnp.concatenate(parts, axis=0).T
        for c in range(4):
            out[pl.ds(4 * g + c, blocks, stride=own_cols), :] = turned[c * blocks : (c + 1) * blocks]


def update_kernel(got, state, adjoint, new_state, new_adjoint):
    steps, planes, rows, cols = state.shape
    for tile in range(cols // LANES):
        block = got[pl.ds(tile * LANES, LANES), :].T
        for t in range(steps):
            for f, (old, new) in enumerate(((state, new_state), (adjoint, new_adjoint))):
                for p in range(planes):
                    at = ((t * 2 + f) * planes + p) * rows
                    new[t, p, :, pl.ds(tile * LANES, LANES)] = (
                        old[t, p, :, pl.ds(tile * LANES, LANES)] + block[at : at + rows]
                    )


def call(kernel, outs, scratch, flops, moved, *args):
    single = not isinstance(outs, list)
    return pl.pallas_call(
        kernel,
        out_shape=outs,
        in_specs=[pl.BlockSpec(memory_space=pltpu.VMEM)] * len(args),
        out_specs=pl.BlockSpec(memory_space=pltpu.VMEM) if single else [pl.BlockSpec(memory_space=pltpu.VMEM)] * len(outs),
        scratch_shapes=scratch,
        compiler_params=pltpu.CompilerParams(vmem_limit_bytes=VMEM_LIMIT),
        cost_estimate=pl.CostEstimate(flops=flops, bytes_accessed=moved, transcendentals=0),
    )(*args)


def f32(*shape):
    return jax.ShapeDtypeStruct(shape, jnp.float32)


def shift(block, axis, distance, wrap):
    count = lax.axis_size(axis)
    route = [(i, (i + distance) % count) for i in range(count) if wrap or 0 <= i + distance < count]
    return lax.ppermute(block, axis, route)


def body(state, adjoint, source, target, conductivity):
    steps, planes, rows, cols = state.shape
    blocks = lax.axis_size("tm")
    me = lax.axis_index("tm")
    own_cols = cols // blocks
    span = own_cols + 2 * WIDE
    half = span // 2
    depth = 2 * planes

    forward, inverse, shifts = transforms(steps * blocks)
    forward = forward.reshape(blocks, steps * 2, LANES).transpose(1, 0, 2)
    wide_forward = np.einsum("tis,cd->tcids", forward, np.eye(4)).reshape(4 * LANES, 4 * LANES)
    inverse = inverse.reshape(LANES, blocks, steps * 2).transpose(0, 2, 1)
    wide_inverse = np.einsum("sti,cd->cstdi", inverse, np.eye(4)).reshape(4 * LANES, 4 * LANES)
    forward_high, forward_low = split_const(wide_forward)
    inverse_high, inverse_low = split_const(wide_inverse)

    padded = jnp.pad(conductivity, ((0, 0), (0, 0), (WIDE, WIDE)))
    slab = lax.dynamic_slice(padded, (0, 0, me * own_cols), (planes, rows, span))
    slab_rows = jnp.pad(slab, ((0, 0), (0, 0), (0, LANES - span))).reshape(planes * rows * LANES // cols, cols)

    def edge(r):
        both = jnp.stack([state[:, :, r], adjoint[:, :, r]]).reshape(2 * steps * planes, cols)
        return jnp.concatenate([both, conductivity[:, r], slab_rows], axis=0)

    top = shift(edge(rows - 1), "space", 1, False)
    bottom = shift(edge(0), "space", -1, False)
    prior = shift(state[-1], "tm", 1, True)
    later = shift(adjoint[0], "tm", -1, True)

    sent = call(
        functools.partial(residual_kernel, blocks),
        f32(blocks, span, LANES),
        [pltpu.VMEM((LANES, cols), jnp.float32), pltpu.VMEM((cols + 2 * WIDE, LANES), jnp.float32)],
        10**7,
        3 * 10**6,
        state, adjoint, source, target, prior, later, top, bottom, conductivity,
    )
    got = lax.all_to_all(sent, "tm", 0, 0, tiled=True).reshape(blocks * span, LANES)
    line = half * depth
    own, up, down = call(
        functools.partial(forward_kernel, (blocks, span, planes, rows)),
        [f32(rows * line, LANES), f32(DEEP * line, LANES), f32(DEEP * line, LANES)],
        [pltpu.VMEM((span // 4 * planes * rows, 4 * LANES), jnp.float32)],
        6 * 10**8,
        4 * 10**6,
        got, forward_high, forward_low,
    )
    above = shift(down, "space", 1, False)
    below = shift(up, "space", -1, False)

    def unpack(packed):
        return packed[-slab_rows.shape[0]:].reshape(planes, rows, LANES)[..., :span]

    kappa = jnp.concatenate([unpack(top), slab, unpack(bottom)], axis=1)
    kappa = kappa.reshape(planes, 3 * rows, 2, half).transpose(1, 3, 2, 0).reshape(3 * rows, half, depth, 1)
    kappa = jnp.broadcast_to(kappa, (3 * rows, half, depth, LANES))
    tall = rows + 2 * DEEP
    tile = (half, depth, LANES)
    back = call(
        functools.partial(sweep_kernel, (blocks, half, planes, rows)),
        f32(blocks * own_cols, LANES),
        [pltpu.VMEM((tall, *tile), jnp.float32)] * 9
        + [pltpu.VMEM((own_cols // 4 * planes * rows, 4 * LANES), jnp.float32)],
        10**9,
        6 * 10**6,
        own.reshape(rows, *tile), above.reshape(DEEP, *tile), below.reshape(DEEP, *tile), kappa, shifts, inverse_high, inverse_low,
    )
    got_back = lax.all_to_all(back, "tm", 0, 0, tiled=True)
    return tuple(
        call(update_kernel, [f32(*state.shape), f32(*state.shape)], [], 10**6, 2 * 10**6, got_back, state, adjoint)
    )


def solution(mesh):
    split = P("tm", None, "space", None)
    return jax.shard_map(
        body,
        mesh=mesh,
        in_specs=(split, split, split, split, P(None, "space", None)),
        out_specs=(split, split),
        check_vma=False,
    )
```

```python
import functools
import math

import jax
import jax.numpy as jnp
import ml_dtypes
import numpy as np
from jax import lax
from jax.experimental import pallas as pl
from jax.experimental.pallas import tpu as pltpu
from jax.sharding import PartitionSpec as P

SWEEPS = 8
STEP = 0.5
PENALTY = 0.05
LANES = 128
WIDE = 8
DEEP = SWEEPS - 1
SUBLANES = 8
VMEM_LIMIT = 28 * 1024 * 1024


def transforms(period):
    q = STEP / PENALTY
    time = np.arange(period)
    pairs = [(0, 1)] + [(k, s) for k in range(1, period // 2) for s in (1, -1)] + [(period // 2, 1)]
    count = len(pairs)
    forward = np.zeros((period, 2, 2 * count))
    inverse = np.zeros((2 * count, period, 2))
    real_shift, imag_shift = np.zeros(count), np.zeros(count)
    for m, (k, sign) in enumerate(pairs):
        theta = 2.0 * math.pi * k / period
        sine = 0.0 if k in (0, period // 2) else math.sin(theta)
        root = math.sqrt(sine * sine + STEP * q)
        real_shift[m] = 1.0 - math.cos(theta)
        imag_shift[m] = sign * root
        wave = np.exp(-1j * theta * time)
        first = (root + sign * sine) / (2.0 * q * root) * wave
        second = -sign * 1j / (2.0 * root) * wave
        for f, row in enumerate((first, second)):
            forward[:, f, m] = row.real
            forward[:, f, count + m] = row.imag
        weight = 2.0 / period
        back = np.conj(wave) * weight
        for f, factor in enumerate((q, sign * 1j * (root - sign * sine))):
            inverse[m, :, f] = (factor * back).real
            inverse[count + m, :, f] = -(factor * back).imag
    real_lane = np.concatenate([real_shift, real_shift])
    imag_lane = np.concatenate([imag_shift, -imag_shift])
    return forward, inverse, np.stack([real_lane, imag_lane]).astype(np.float32)


def split_const(matrix):
    high = matrix.astype(np.float32).astype(ml_dtypes.bfloat16)
    low = (matrix - high.astype(np.float64)).astype(np.float32).astype(ml_dtypes.bfloat16)
    return high, low


def dot_split(left, high_ref, low_ref):
    high = left.astype(jnp.bfloat16)
    low = (left - high.astype(jnp.float32)).astype(jnp.bfloat16)
    dot = functools.partial(jnp.dot, preferred_element_type=jnp.float32)
    return dot(high, high_ref[...]) + (dot(low, high_ref[...]) + dot(high, low_ref[...]))


def pack_kernel(own_cols, me, state, adjoint, cond, to_down, to_up, last, first):
    steps, planes, rows, cols = state.shape
    tiles = cols // LANES
    per_tile = 2 * steps * planes
    for out, r in ((to_down, rows - 1), (to_up, 0)):
        for k in range(tiles):
            lanes = pl.ds(k * LANES, LANES)
            for f, field in enumerate((state, adjoint)):
                for t in range(steps):
                    for p in range(planes):
                        out[pl.ds(k * per_tile + (f * steps + t) * planes + p, 1), :] = field[t, p, pl.ds(r, 1), lanes]
            for p in range(planes):
                out[pl.ds(tiles * per_tile + k * planes + p, 1), :] = cond[p, pl.ds(r, 1), lanes]
    start = me[0] * own_cols - WIDE
    column = lax.broadcasted_iota(jnp.int32, (rows, LANES), 1) + start
    base = tiles * (per_tile + planes)
    for p in range(planes):
        turned = pltpu.roll(cond[p], lax.rem(cols - start, cols), axis=1)[:, :LANES]
        slab = jnp.where((column >= 0) & (column < cols), turned, 0.0)
        to_down[pl.ds(base + p * rows, rows), :] = slab
        to_up[pl.ds(base + p * rows, rows), :] = slab
    last[...] = state[steps - 1]
    first[...] = adjoint[0]


def edge_row(packed, tiles, base, stride, at):
    return jnp.concatenate([packed[pl.ds(base + k * stride + at, 1), :] for k in range(tiles)], axis=1)


def local_kernel(state, adjoint, source, target, cond, out):
    steps, planes, rows, cols = state.shape
    row = lax.broadcasted_iota(jnp.int32, (rows, cols), 0)
    col = lax.broadcasted_iota(jnp.int32, (rows, cols), 1)

    def near(value):
        return (
            pltpu.roll(value, 1, axis=0),
            pltpu.roll(value, rows - 1, axis=0),
            jnp.where(col == 0, 0.0, pltpu.roll(value, 1, axis=1)),
            jnp.where(col == cols - 1, 0.0, pltpu.roll(value, cols - 1, axis=1)),
        )

    kappa = [cond[p] for p in range(planes)]
    zero = jnp.zeros((rows, cols), jnp.float32)
    for p in range(planes):
        around = near(kappa[p])
        around += (kappa[p - 1] if p else zero, kappa[p + 1] if p < planes - 1 else zero)
        weights = [(0.5 * STEP) * (kappa[p] + k) for k in around]
        weights[0] = jnp.where(row == 0, 0.0, weights[0])
        weights[1] = jnp.where(row == rows - 1, 0.0, weights[1])
        diag = weights[0]
        for w in weights[1:]:
            diag = diag + w
        for t in range(steps):
            stiff = []
            for field in (state, adjoint):
                value = field[t, p]
                total = diag * value
                for w, v in zip(weights, near(value)):
                    total = total - w * v
                if p:
                    total = total - weights[4] * field[t, p - 1]
                if p < planes - 1:
                    total = total - weights[5] * field[t, p + 1]
                stiff.append(total)
            s, a = state[t, p], adjoint[t, p]
            s_step = s - state[t - 1, p] if t else s
            a_step = a - adjoint[t + 1, p] if t < steps - 1 else a
            first = STEP * source[t, p] - (s_step + stiff[0] + (STEP / PENALTY) * a)
            second = -STEP * target[t, p] - (a_step + stiff[1] - STEP * s)
            for f, value in enumerate((first, second)):
                out[pl.ds(((t * 2 + f) * planes + p) * rows, rows), :] = value


def finish_kernel(blocks, partial, state, adjoint, prior, later, top, bottom, cond, out, res, turned):
    steps, planes, rows, cols = state.shape
    tiles = cols // LANES
    per_tile = 2 * steps * planes
    row = lax.broadcasted_iota(jnp.int32, (rows, cols), 0)
    for p in range(planes):
        weights = []
        for packed, r in ((top, 0), (bottom, rows - 1)):
            beyond = edge_row(packed, tiles, tiles * per_tile, planes, p)
            weights.append(jnp.where(row == r, (0.5 * STEP) * (cond[p] + beyond), 0.0))
        for t in range(steps):
            for f, field in enumerate((state, adjoint)):
                at = ((t * 2 + f) * planes + p) * rows
                edge = (f * steps + t) * planes + p
                value = field[t, p]
                total = partial[pl.ds(at, rows), :]
                for packed, w in zip((top, bottom), weights):
                    total = total - w * (value - edge_row(packed, tiles, 0, per_tile, edge))
                if f == 0 and t == 0:
                    total = total + prior[p]
                if f == 1 and t == steps - 1:
                    total = total + later[p]
                res[pl.ds(at, rows), :] = total
    turned[pl.ds(0, WIDE), :] = jnp.zeros((WIDE, LANES), jnp.float32)
    turned[pl.ds(WIDE + cols, WIDE), :] = jnp.zeros((WIDE, LANES), jnp.float32)
    for tile in range(tiles):
        turned[pl.ds(WIDE + tile * LANES, LANES), :] = res[:, pl.ds(tile * LANES, LANES)].T
    own = cols // blocks
    for j in range(blocks):
        out[j] = turned[pl.ds(j * own, own + 2 * WIDE), :]


def column_group(g, span):
    near = [2 * g, 2 * g + 1]
    return near + [span - 1 - c for c in near]


def forward_kernel(shape, got, high, low, own, up, down, left):
    blocks, span, planes, rows = shape
    strip = span // (2 * SUBLANES)
    line = planes * span
    cells = planes * rows
    for g in range(span // 4):
        parts = [got[pl.ds(c, blocks, stride=span), :] for c in column_group(g, span)]
        turned = jnp.concatenate(parts, axis=0).T
        for tf in range(4):
            left[pl.ds(g * cells, cells), pl.ds(tf * LANES, LANES)] = turned[tf * cells : (tf + 1) * cells]
    spectrum = dot_split(left[...], high, low)
    for g in range(span // 4):
        for pair in range(2):
            sub, at = divmod(2 * g + pair, strip)
            for part in range(2):
                lane = (2 * pair + part) * LANES
                for p in range(planes):
                    piece = spectrum[g * cells + p * rows : g * cells + (p + 1) * rows, lane : lane + LANES]
                    begin = ((p * strip + at) * 2 + part) * SUBLANES + sub
                    own[pl.ds(begin, rows, stride=line), :] = piece
    up[...] = own[pl.ds(0, line * DEEP), :]
    down[...] = own[pl.ds(line, line * DEEP), :]


def weight_kernel(shape, kappa, shifts, w_row, w_col, w_plane, scale, cross, wide):
    planes, strip = shape
    count = planes * strip
    tall = scale.shape[0]
    sub = lax.broadcasted_iota(jnp.int32, (SUBLANES, LANES), 0)
    mirrored = lax.broadcasted_iota(jnp.int32, (SUBLANES, LANES), 1) >= LANES // 2
    real = jnp.broadcast_to(shifts[0:1, :], (SUBLANES, LANES))
    imag = jnp.broadcast_to(shifts[1:2, :], (SUBLANES, LANES))

    def spread(r, _):
        packed = kappa[r]
        for n in range(count):
            a = jnp.broadcast_to(packed[:, n : n + 1], (SUBLANES, LANES))
            b = jnp.broadcast_to(packed[:, count + n : count + n + 1], (SUBLANES, LANES))
            wide[r, n] = jnp.where(mirrored, b, a)

    def bond(a, b):
        return jnp.where(a * b > 0.0, (0.5 * STEP) * (a + b), 0.0)

    def setup(r, _):
        here = [wide[r + 1, n] for n in range(count)]
        for p in range(planes):
            for c in range(strip):
                n = p * strip + c
                mine = here[n]
                if c:
                    to_left = here[n - 1]
                else:
                    to_left = jnp.where(sub == 0, 0.0, pltpu.roll(here[n + strip - 1], 1, axis=0))
                    w_col[r, p * (strip + 1)] = bond(mine, to_left)
                if c < strip - 1:
                    to_right = here[n + 1]
                else:
                    to_right = pltpu.roll(here[n - strip + 1], SUBLANES - 1, axis=0)
                    to_right = jnp.where(sub == SUBLANES - 1, pltpu.roll(mine, LANES // 2, axis=1), to_right)
                w_col[r, p * (strip + 1) + c + 1] = bond(mine, to_right)
                below = wide[r + 2, n]
                w_row[r, n] = bond(mine, below)
                around = wide[r, n] + below + to_left + to_right
                if p:
                    around = around + here[n - strip]
                if p < planes - 1:
                    around = around + here[n + strip]
                    w_plane[r, n] = bond(mine, here[n + strip])
                big = (0.5 * STEP) * (6.0 * mine + around) + real
                inv = 1.0 / (big * big + imag * imag)
                scale[r, n] = big * inv
                cross[r, n] = imag * inv

    lax.fori_loop(0, tall + 2, spread, None)
    lax.fori_loop(0, tall, setup, None)


def sweep_kernel(shape, own, above, below, w_row, w_col, w_plane, scale, cross, high, low, out, rhs, first, second, left):
    blocks, own_cols, planes, strip = shape
    rows = own.shape[0]
    tall = rows + 2 * DEEP
    count = planes * strip
    line = 2 * count * SUBLANES
    sub = lax.broadcasted_iota(jnp.int32, (SUBLANES, LANES), 0)

    def at(r, n):
        return pl.ds(pl.multiple_of((r * 2 * count + n) * SUBLANES, SUBLANES), SUBLANES)

    def solve(target, totals, r, m):
        a, b = scale[r, m], cross[r, m]
        target[at(r, 2 * m), :] = a * totals[0] + b * totals[1]
        target[at(r, 2 * m + 1), :] = a * totals[1] - b * totals[0]

    for source, offset in ((above, 0), (own, DEEP), (below, DEEP + rows)):

        def start(r, _, source=source, offset=offset):
            for m in range(count):
                pair = [source[r, 2 * m + k] for k in range(2)]
                for k in range(2):
                    rhs[r + offset, 2 * m + k] = pair[k]
                solve(first, pair, r + offset, m)

        lax.fori_loop(0, source.shape[0], start, None)

    def relax(old, new, r):
        here = [[old[at(r, 2 * m + k), :] for k in range(2)] for m in range(count)]
        for p in range(planes):
            base = p * strip
            before = [pltpu.roll(v, 1, axis=0) for v in here[base + strip - 1]]
            across = [pltpu.roll(v, LANES // 2, axis=1) for v in here[base + strip - 1]]
            after = [pltpu.roll(v, SUBLANES - 1, axis=0) for v in here[base]]
            after = [jnp.where(sub == SUBLANES - 1, x, v) for x, v in zip(across, after)]
            for c in range(strip):
                m = base + c
                flank = p * (strip + 1) + c
                totals = []
                for k in range(2):
                    to_left = here[m - 1][k] if c else before[k]
                    to_right = here[m + 1][k] if c < strip - 1 else after[k]
                    total = w_col[r, flank] * to_left + w_col[r, flank + 1] * to_right
                    others = w_row[r, m] * old[at(r + 1, 2 * m + k), :] + w_row[r - 1, m] * old[at(r - 1, 2 * m + k), :]
                    mine = rhs[r, 2 * m + k]
                    if p:
                        mine = mine + w_plane[r, m - strip] * here[m - strip][k]
                    if p < planes - 1:
                        others = others + w_plane[r, m] * here[m + strip][k]
                    totals.append(mine + (total + others))
                solve(new, totals, r, m)

    old, new = first, second
    for sweep in range(1, SWEEPS):

        def step(q, _, old=old, new=new, sweep=sweep):
            relax(old, new, sweep + 2 * q)
            relax(old, new, sweep + 2 * q + 1)

        lax.fori_loop(0, (tall - 2 * sweep) // 2, step, None)
        old, new = new, old

    cells = planes * rows
    for g in range(own_cols // 4):
        for pair in range(2):
            side, place = divmod(2 * g + pair + WIDE, strip)
            for part in range(2):
                for p in range(planes):
                    begin = DEEP * line + ((p * strip + place) * 2 + part) * SUBLANES + side
                    piece = old[pl.ds(begin, rows, stride=line), :]
                    left[pl.ds(g * cells + p * rows, rows), pl.ds((2 * pair + part) * LANES, LANES)] = piece
    values = dot_split(left[...], high, low)
    for g in range(own_cols // 4):
        parts = [values[g * cells : (g + 1) * cells, tf * LANES : (tf + 1) * LANES] for tf in range(4)]
        turned = jnp.concatenate(parts, axis=0).T
        for c, column in enumerate(column_group(g, own_cols)):
            out[pl.ds(column, blocks, stride=own_cols), :] = turned[c * blocks : (c + 1) * blocks]


def update_kernel(got, state, adjoint, new_state, new_adjoint):
    steps, planes, rows, cols = state.shape
    for tile in range(cols // LANES):
        block = got[pl.ds(tile * LANES, LANES), :].T
        for t in range(steps):
            for f, (old, new) in enumerate(((state, new_state), (adjoint, new_adjoint))):
                for p in range(planes):
                    at = ((t * 2 + f) * planes + p) * rows
                    new[t, p, :, pl.ds(tile * LANES, LANES)] = (
                        old[t, p, :, pl.ds(tile * LANES, LANES)] + block[at : at + rows]
                    )


def call(kernel, outs, scratch, flops, moved, *args, scalars=0):
    vmem = pl.BlockSpec(memory_space=pltpu.VMEM)
    smem = pl.BlockSpec(memory_space=pltpu.SMEM)
    return pl.pallas_call(
        kernel,
        out_shape=outs,
        in_specs=[smem] * scalars + [vmem] * (len(args) - scalars),
        out_specs=[vmem] * len(outs) if isinstance(outs, list) else vmem,
        scratch_shapes=scratch,
        compiler_params=pltpu.CompilerParams(vmem_limit_bytes=VMEM_LIMIT),
        cost_estimate=pl.CostEstimate(flops=flops, bytes_accessed=moved, transcendentals=0),
    )(*args)


def f32(*shape):
    return jax.ShapeDtypeStruct(shape, jnp.float32)


def shift(block, axis, distance, wrap):
    count = lax.axis_size(axis)
    route = [(i, (i + distance) % count) for i in range(count) if wrap or 0 <= i + distance < count]
    return lax.ppermute(block, axis, route)


def body(state, adjoint, source, target, conductivity):
    steps, planes, rows, cols = state.shape
    blocks = lax.axis_size("tm")
    me = lax.axis_index("tm")
    own_cols = cols // blocks
    span = own_cols + 2 * WIDE
    strip = span // (2 * SUBLANES)
    count = planes * strip
    line = 2 * count * SUBLANES
    tall = rows + 2 * DEEP
    tiles = cols // LANES
    tile = (SUBLANES, LANES)

    forward, inverse, shifts = transforms(steps * blocks)
    same = np.eye(4).reshape(4, 2, 2)
    forward = forward.reshape(blocks, steps * 2, 2, LANES // 2)
    forward = np.einsum("itks,chp->tcipkhs", forward, same).reshape(4 * LANES, 4 * LANES)
    inverse = inverse.reshape(2, LANES // 2, blocks, steps * 2)
    inverse = np.einsum("ksit,chp->pkhstci", inverse, same).reshape(4 * LANES, 4 * LANES)
    forward_high, forward_low = split_const(forward)
    inverse_high, inverse_low = split_const(inverse)

    edges = tiles * planes * (2 * steps + 1) + planes * rows
    to_down, to_up, last, first = call(
        functools.partial(pack_kernel, own_cols),
        [f32(edges, LANES), f32(edges, LANES), f32(planes, rows, cols), f32(planes, rows, cols)],
        [],
        10**5,
        10**6,
        me.reshape(1), state, adjoint, conductivity,
        scalars=1,
    )
    top = shift(to_down, "space", 1, False)
    bottom = shift(to_up, "space", -1, False)
    prior = shift(last, "tm", 1, True)
    later = shift(first, "tm", -1, True)
    partial = call(
        local_kernel,
        f32(LANES, cols),
        [],
        10**7,
        3 * 10**6,
        state, adjoint, source, target, conductivity,
    )
    sent = call(
        functools.partial(finish_kernel, blocks),
        f32(blocks, span, LANES),
        [pltpu.VMEM((LANES, cols), jnp.float32), pltpu.VMEM((cols + 2 * WIDE, LANES), jnp.float32)],
        10**7,
        3 * 10**6,
        partial, state, adjoint, prior, later, top, bottom, conductivity,
    )
    got = lax.all_to_all(sent, "tm", 0, 0, tiled=True).reshape(blocks * span, LANES)
    own, up, down = call(
        functools.partial(forward_kernel, (blocks, span, planes, rows)),
        [f32(rows * line, LANES), f32(DEEP * line, LANES), f32(DEEP * line, LANES)],
        [pltpu.VMEM((span // 4 * planes * rows, 4 * LANES), jnp.float32)],
        6 * 10**8,
        4 * 10**6,
        got, forward_high, forward_low,
    )
    above = shift(down, "space", 1, False)
    below = shift(up, "space", -1, False)

    def unpack(packed):
        return packed[edges - planes * rows :].reshape(planes, rows, LANES)[..., :span]

    kappa = jnp.concatenate([unpack(top), unpack(to_up), unpack(bottom)], axis=1)
    kappa = jnp.stack([kappa[..., : span // 2], kappa[..., : span // 2 - 1 : -1]], axis=2)
    kappa = kappa.reshape(planes, 3 * rows, 2, SUBLANES, strip).transpose(1, 3, 2, 0, 4).reshape(3 * rows, SUBLANES, 2 * count)
    kappa = jnp.pad(kappa, ((0, 0), (0, 0), (0, LANES - 2 * count)))
    weights = call(
        functools.partial(weight_kernel, (planes, strip)),
        [
            f32(tall, count, *tile),
            f32(tall, planes * (strip + 1), *tile),
            f32(tall, count - strip, *tile),
            f32(tall, count, *tile),
            f32(tall, count, *tile),
        ],
        [pltpu.VMEM((3 * rows, count, *tile), jnp.float32)],
        10**9,
        10**7,
        kappa, np.tile(shifts.reshape(2, 2, -1)[:, :1], (1, 2, 1)).reshape(2, LANES),
    )
    back = call(
        functools.partial(sweep_kernel, (blocks, own_cols, planes, strip)),
        f32(blocks * own_cols, LANES),
        [
            pltpu.VMEM((tall, 2 * count, *tile), jnp.float32),
            pltpu.VMEM((tall * line, LANES), jnp.float32),
            pltpu.VMEM((tall * line, LANES), jnp.float32),
            pltpu.VMEM((own_cols // 4 * planes * rows, 4 * LANES), jnp.float32),
        ],
        10**9,
        6 * 10**6,
        own.reshape(rows, 2 * count, *tile), above.reshape(DEEP, 2 * count, *tile), below.reshape(DEEP, 2 * count, *tile),
        *weights, inverse_high, inverse_low,
    )
    got_back = lax.all_to_all(back, "tm", 0, 0, tiled=True)
    return tuple(
        call(update_kernel, [f32(*state.shape), f32(*state.shape)], [], 10**6, 2 * 10**6, got_back, state, adjoint)
    )


def solution(mesh):
    split = P("tm", None, "space", None)
    return jax.shard_map(
        body,
        mesh=mesh,
        in_specs=(split, split, split, split, P(None, "space", None)),
        out_specs=(split, split),
        check_vma=False,
    )
```

```python
import functools
import math

import jax
import jax.numpy as jnp
import ml_dtypes
import numpy as np
from jax import lax
from jax.experimental import pallas as pl
from jax.experimental.pallas import tpu as pltpu
from jax.sharding import PartitionSpec as P

SWEEPS = 8
STEP = 0.5
PENALTY = 0.05
LANES = 128
WIDE = 8
DEEP = SWEEPS - 1
SUBLANES = 8
VMEM_LIMIT = 28 * 1024 * 1024
WHOLE_VMEM = 60 * 1024 * 1024


def transforms(period):
    q = STEP / PENALTY
    time = np.arange(period)
    pairs = [(0, 1)] + [(k, s) for k in range(1, period // 2) for s in (1, -1)] + [(period // 2, 1)]
    count = len(pairs)
    forward = np.zeros((period, 2, 2 * count))
    inverse = np.zeros((2 * count, period, 2))
    real_shift, imag_shift = np.zeros(count), np.zeros(count)
    for m, (k, sign) in enumerate(pairs):
        theta = 2.0 * math.pi * k / period
        sine = 0.0 if k in (0, period // 2) else math.sin(theta)
        root = math.sqrt(sine * sine + STEP * q)
        real_shift[m] = 1.0 - math.cos(theta)
        imag_shift[m] = sign * root
        wave = np.exp(-1j * theta * time)
        first = (root + sign * sine) / (2.0 * q * root) * wave
        second = -sign * 1j / (2.0 * root) * wave
        for f, row in enumerate((first, second)):
            forward[:, f, m] = row.real
            forward[:, f, count + m] = row.imag
        weight = 2.0 / period
        back = np.conj(wave) * weight
        for f, factor in enumerate((q, sign * 1j * (root - sign * sine))):
            inverse[m, :, f] = (factor * back).real
            inverse[count + m, :, f] = -(factor * back).imag
    real_lane = np.concatenate([real_shift, real_shift])
    imag_lane = np.concatenate([imag_shift, -imag_shift])
    return forward, inverse, np.stack([real_lane, imag_lane]).astype(np.float32)


def split_const(matrix):
    high = matrix.astype(np.float32).astype(ml_dtypes.bfloat16)
    low = (matrix - high.astype(np.float64)).astype(np.float32).astype(ml_dtypes.bfloat16)
    return high, low


def dot_split(left, high_ref, low_ref):
    high = left.astype(jnp.bfloat16)
    low = (left - high.astype(jnp.float32)).astype(jnp.bfloat16)
    dot = functools.partial(jnp.dot, preferred_element_type=jnp.float32)
    return dot(high, high_ref[...]) + (dot(low, high_ref[...]) + dot(high, low_ref[...]))


def fetch(sources, targets, sems):
    copies = [pltpu.make_async_copy(x, y, sems.at[i]) for i, (x, y) in enumerate(zip(sources, targets))]
    for copy in copies:
        copy.start()
    return copies


def pack_kernel(own_cols, me, state_far, adjoint_far, cond_far, to_down, to_up, last, first, state, adjoint, cond, sems):
    steps, planes, rows, cols = state.shape
    tiles = cols // LANES
    per_tile = 2 * steps * planes
    for copy in fetch((state_far, adjoint_far, cond_far), (state, adjoint, cond), sems):
        copy.wait()
    for out, r in ((to_down, rows - 1), (to_up, 0)):
        for k in range(tiles):
            lanes = pl.ds(k * LANES, LANES)
            for f, field in enumerate((state, adjoint)):
                for t in range(steps):
                    for p in range(planes):
                        out[pl.ds(k * per_tile + (f * steps + t) * planes + p, 1), :] = field[t, p, pl.ds(r, 1), lanes]
            for p in range(planes):
                out[pl.ds(tiles * per_tile + k * planes + p, 1), :] = cond[p, pl.ds(r, 1), lanes]
    start = me[0] * own_cols - WIDE
    column = lax.broadcasted_iota(jnp.int32, (rows, LANES), 1) + start
    base = tiles * (per_tile + planes)
    for p in range(planes):
        turned = pltpu.roll(cond[p], lax.rem(cols - start, cols), axis=1)[:, :LANES]
        slab = jnp.where((column >= 0) & (column < cols), turned, 0.0)
        to_down[pl.ds(base + p * rows, rows), :] = slab
        to_up[pl.ds(base + p * rows, rows), :] = slab
    last[...] = state[steps - 1]
    first[...] = adjoint[0]


def edge_row(packed, tiles, base, stride, at):
    return jnp.concatenate([packed[pl.ds(base + k * stride + at, 1), :] for k in range(tiles)], axis=1)


def local_kernel(*refs):
    count = 5
    out, sems = refs[count], refs[-1]
    state, adjoint, source, target, cond = refs[count + 1 : 2 * count + 1]
    for copy in fetch(refs[:count], refs[count + 1 : 2 * count + 1], sems):
        copy.wait()
    steps, planes, rows, cols = state.shape
    row = lax.broadcasted_iota(jnp.int32, (rows, cols), 0)
    col = lax.broadcasted_iota(jnp.int32, (rows, cols), 1)

    def near(value):
        return (
            pltpu.roll(value, 1, axis=0),
            pltpu.roll(value, rows - 1, axis=0),
            jnp.where(col == 0, 0.0, pltpu.roll(value, 1, axis=1)),
            jnp.where(col == cols - 1, 0.0, pltpu.roll(value, cols - 1, axis=1)),
        )

    kappa = [cond[p] for p in range(planes)]
    zero = jnp.zeros((rows, cols), jnp.float32)
    for p in range(planes):
        around = near(kappa[p])
        around += (kappa[p - 1] if p else zero, kappa[p + 1] if p < planes - 1 else zero)
        weights = [(0.5 * STEP) * (kappa[p] + k) for k in around]
        weights[0] = jnp.where(row == 0, 0.0, weights[0])
        weights[1] = jnp.where(row == rows - 1, 0.0, weights[1])
        diag = weights[0]
        for w in weights[1:]:
            diag = diag + w
        for t in range(steps):
            stiff = []
            for field in (state, adjoint):
                value = field[t, p]
                total = diag * value
                for w, v in zip(weights, near(value)):
                    total = total - w * v
                if p:
                    total = total - weights[4] * field[t, p - 1]
                if p < planes - 1:
                    total = total - weights[5] * field[t, p + 1]
                stiff.append(total)
            s, a = state[t, p], adjoint[t, p]
            s_step = s - state[t - 1, p] if t else s
            a_step = a - adjoint[t + 1, p] if t < steps - 1 else a
            first = STEP * source[t, p] - (s_step + stiff[0] + (STEP / PENALTY) * a)
            second = -STEP * target[t, p] - (a_step + stiff[1] - STEP * s)
            for f, value in enumerate((first, second)):
                out[pl.ds(((t * 2 + f) * planes + p) * rows, rows), :] = value


def finish_kernel(shape, place, partial, to_down, to_up, prior, later, top, bottom, out, res, turned):
    blocks, steps, planes, rows, ends = shape
    cols = partial.shape[1]
    tiles = cols // LANES
    per_tile = 2 * steps * planes
    row = lax.broadcasted_iota(jnp.int32, (rows, cols), 0)
    inside = [jnp.where(place[0] == end, 0.0, 1.0) for end in ends]
    sides = ((0, to_up, top), (rows - 1, to_down, bottom))
    for p in range(planes):
        weights = []
        for i, (_, mine, other) in enumerate(sides):
            here = edge_row(mine, tiles, tiles * per_tile, planes, p)
            beyond = edge_row(other, tiles, tiles * per_tile, planes, p)
            weights.append((0.5 * STEP) * (here + beyond * inside[i]))
        for t in range(steps):
            for f in range(2):
                at = ((t * 2 + f) * planes + p) * rows
                edge = (f * steps + t) * planes + p
                total = partial[pl.ds(at, rows), :]
                for i, (r, mine, other) in enumerate(sides):
                    here = edge_row(mine, tiles, 0, per_tile, edge)
                    beyond = edge_row(other, tiles, 0, per_tile, edge)
                    total = jnp.where(row == r, total - weights[i] * (here - beyond * inside[i]), total)
                if f == 0 and t == 0:
                    total = total + prior[p]
                if f == 1 and t == steps - 1:
                    total = total + later[p]
                res[pl.ds(at, rows), :] = total
    turned[pl.ds(0, WIDE), :] = jnp.zeros((WIDE, LANES), jnp.float32)
    turned[pl.ds(WIDE + cols, WIDE), :] = jnp.zeros((WIDE, LANES), jnp.float32)
    for tile in range(tiles):
        turned[pl.ds(WIDE + tile * LANES, LANES), :] = res[:, pl.ds(tile * LANES, LANES)].T
    own = cols // blocks
    for j in range(blocks):
        out[j] = turned[pl.ds(j * own, own + 2 * WIDE), :]


def column_group(g, span):
    near = [2 * g, 2 * g + 1]
    return near + [span - 1 - c for c in near]


def forward_kernel(shape, got, high_far, low_far, own, up, down, left, high, low, sems):
    blocks, span, planes, rows = shape
    copies = fetch((high_far, low_far), (high, low), sems)
    strip = span // (2 * SUBLANES)
    line = planes * span
    cells = planes * rows
    for g in range(span // 4):
        parts = [got[pl.ds(c, blocks, stride=span), :] for c in column_group(g, span)]
        turned = jnp.concatenate(parts, axis=0).T
        for tf in range(4):
            left[pl.ds(g * cells, cells), pl.ds(tf * LANES, LANES)] = turned[tf * cells : (tf + 1) * cells]
    for copy in copies:
        copy.wait()
    spectrum = dot_split(left[...], high, low)
    for g in range(span // 4):
        for pair in range(2):
            sub, at = divmod(2 * g + pair, strip)
            for part in range(2):
                lane = (2 * pair + part) * LANES
                for p in range(planes):
                    piece = spectrum[g * cells + p * rows : g * cells + (p + 1) * rows, lane : lane + LANES]
                    begin = ((p * strip + at) * 2 + part) * SUBLANES + sub
                    own[pl.ds(begin, rows, stride=line), :] = piece
    up[...] = own[pl.ds(0, line * DEEP), :]
    down[...] = own[pl.ds(line, line * DEEP), :]


def weight_kernel(shape, kappa, shifts, w_row, w_col, w_plane, scale, cross, wide):
    planes, strip = shape
    count = planes * strip
    tall = scale.shape[0]
    sub = lax.broadcasted_iota(jnp.int32, (SUBLANES, LANES), 0)
    mirrored = lax.broadcasted_iota(jnp.int32, (SUBLANES, LANES), 1) >= LANES // 2
    real = jnp.broadcast_to(shifts[0:1, :], (SUBLANES, LANES))
    imag = jnp.broadcast_to(shifts[1:2, :], (SUBLANES, LANES))

    def spread(r, _):
        packed = kappa[r]
        for n in range(count):
            a = jnp.broadcast_to(packed[:, n : n + 1], (SUBLANES, LANES))
            b = jnp.broadcast_to(packed[:, count + n : count + n + 1], (SUBLANES, LANES))
            wide[r, n] = jnp.where(mirrored, b, a)

    def bond(a, b):
        return jnp.where(a * b > 0.0, (0.5 * STEP) * (a + b), 0.0)

    def setup(r, _):
        here = [wide[r + 1, n] for n in range(count)]
        for p in range(planes):
            for c in range(strip):
                n = p * strip + c
                mine = here[n]
                if c:
                    to_left = here[n - 1]
                else:
                    to_left = jnp.where(sub == 0, 0.0, pltpu.roll(here[n + strip - 1], 1, axis=0))
                    w_col[r, p * (strip + 1)] = bond(mine, to_left)
                if c < strip - 1:
                    to_right = here[n + 1]
                else:
                    to_right = pltpu.roll(here[n - strip + 1], SUBLANES - 1, axis=0)
                    to_right = jnp.where(sub == SUBLANES - 1, pltpu.roll(mine, LANES // 2, axis=1), to_right)
                w_col[r, p * (strip + 1) + c + 1] = bond(mine, to_right)
                below = wide[r + 2, n]
                w_row[r, n] = bond(mine, below)
                around = wide[r, n] + below + to_left + to_right
                if p:
                    around = around + here[n - strip]
                if p < planes - 1:
                    around = around + here[n + strip]
                    w_plane[r, n] = bond(mine, here[n + strip])
                big = (0.5 * STEP) * (6.0 * mine + around) + real
                inv = 1.0 / (big * big + imag * imag)
                scale[r, n] = big * inv
                cross[r, n] = imag * inv

    lax.fori_loop(0, tall + 2, spread, None)
    lax.fori_loop(0, tall, setup, None)


def sweep_kernel(shape, own, above, below, w_row, w_col, w_plane, scale, cross, high, low, out, rhs, first, second, left):
    blocks, own_cols, planes, strip = shape
    rows = own.shape[0]
    tall = rows + 2 * DEEP
    count = planes * strip
    line = 2 * count * SUBLANES
    sub = lax.broadcasted_iota(jnp.int32, (SUBLANES, LANES), 0)

    def at(r, n):
        return pl.ds(pl.multiple_of((r * 2 * count + n) * SUBLANES, SUBLANES), SUBLANES)

    def solve(target, totals, r, m):
        a, b = scale[r, m], cross[r, m]
        target[at(r, 2 * m), :] = a * totals[0] + b * totals[1]
        target[at(r, 2 * m + 1), :] = a * totals[1] - b * totals[0]

    for source, offset in ((above, 0), (own, DEEP), (below, DEEP + rows)):

        def start(r, _, source=source, offset=offset):
            for m in range(count):
                pair = [source[r, 2 * m + k] for k in range(2)]
                for k in range(2):
                    rhs[r + offset, 2 * m + k] = pair[k]
                solve(first, pair, r + offset, m)

        lax.fori_loop(0, source.shape[0], start, None)

    def relax(old, new, r):
        here = [[old[at(r, 2 * m + k), :] for k in range(2)] for m in range(count)]
        for p in range(planes):
            base = p * strip
            before = [pltpu.roll(v, 1, axis=0) for v in here[base + strip - 1]]
            across = [pltpu.roll(v, LANES // 2, axis=1) for v in here[base + strip - 1]]
            after = [pltpu.roll(v, SUBLANES - 1, axis=0) for v in here[base]]
            after = [jnp.where(sub == SUBLANES - 1, x, v) for x, v in zip(across, after)]
            for c in range(strip):
                m = base + c
                flank = p * (strip + 1) + c
                totals = []
                for k in range(2):
                    to_left = here[m - 1][k] if c else before[k]
                    to_right = here[m + 1][k] if c < strip - 1 else after[k]
                    total = w_col[r, flank] * to_left + w_col[r, flank + 1] * to_right
                    others = w_row[r, m] * old[at(r + 1, 2 * m + k), :] + w_row[r - 1, m] * old[at(r - 1, 2 * m + k), :]
                    mine = rhs[r, 2 * m + k]
                    if p:
                        mine = mine + w_plane[r, m - strip] * here[m - strip][k]
                    if p < planes - 1:
                        others = others + w_plane[r, m] * here[m + strip][k]
                    totals.append(mine + (total + others))
                solve(new, totals, r, m)

    old, new = first, second
    for sweep in range(1, SWEEPS):

        def step(q, _, old=old, new=new, sweep=sweep):
            relax(old, new, sweep + 2 * q)
            relax(old, new, sweep + 2 * q + 1)

        lax.fori_loop(0, (tall - 2 * sweep) // 2, step, None)
        old, new = new, old

    cells = planes * rows
    for g in range(own_cols // 4):
        for pair in range(2):
            side, place = divmod(2 * g + pair + WIDE, strip)
            for part in range(2):
                for p in range(planes):
                    begin = DEEP * line + ((p * strip + place) * 2 + part) * SUBLANES + side
                    piece = old[pl.ds(begin, rows, stride=line), :]
                    left[pl.ds(g * cells + p * rows, rows), pl.ds((2 * pair + part) * LANES, LANES)] = piece
    values = dot_split(left[...], high, low)
    for g in range(own_cols // 4):
        parts = [values[g * cells : (g + 1) * cells, tf * LANES : (tf + 1) * LANES] for tf in range(4)]
        turned = jnp.concatenate(parts, axis=0).T
        for c, column in enumerate(column_group(g, own_cols)):
            out[pl.ds(column, blocks, stride=own_cols), :] = turned[c * blocks : (c + 1) * blocks]


def update_kernel(got, state, adjoint, new_state, new_adjoint):
    steps, planes, rows, cols = state.shape
    for tile in range(cols // LANES):
        block = got[pl.ds(tile * LANES, LANES), :].T
        for t in range(steps):
            for f, (old, new) in enumerate(((state, new_state), (adjoint, new_adjoint))):
                for p in range(planes):
                    at = ((t * 2 + f) * planes + p) * rows
                    new[t, p, :, pl.ds(tile * LANES, LANES)] = (
                        old[t, p, :, pl.ds(tile * LANES, LANES)] + block[at : at + rows]
                    )


def call(kernel, outs, scratch, flops, moved, *args, places="", limit=VMEM_LIMIT):
    spaces = {"s": pltpu.SMEM, "h": pltpu.HBM, "v": pltpu.VMEM}
    vmem = pl.BlockSpec(memory_space=pltpu.VMEM)
    return pl.pallas_call(
        kernel,
        out_shape=outs,
        in_specs=[pl.BlockSpec(memory_space=spaces[x]) for x in places.ljust(len(args), "v")],
        out_specs=[vmem] * len(outs) if isinstance(outs, list) else vmem,
        scratch_shapes=scratch,
        compiler_params=pltpu.CompilerParams(vmem_limit_bytes=limit),
        cost_estimate=pl.CostEstimate(flops=flops, bytes_accessed=moved, transcendentals=0),
    )(*args)


def v32(*shape):
    return pltpu.VMEM(shape, jnp.float32)


def f32(*shape):
    return jax.ShapeDtypeStruct(shape, jnp.float32)


def shift(block, axis, distance):
    count = lax.axis_size(axis)
    return lax.ppermute(block, axis, [(i, (i + distance) % count) for i in range(count)])


def body(state, adjoint, source, target, conductivity):
    steps, planes, rows, cols = state.shape
    blocks = lax.axis_size("tm")
    me = lax.axis_index("tm")
    own_cols = cols // blocks
    span = own_cols + 2 * WIDE
    strip = span // (2 * SUBLANES)
    count = planes * strip
    line = 2 * count * SUBLANES
    tall = rows + 2 * DEEP
    tiles = cols // LANES
    tile = (SUBLANES, LANES)

    forward, inverse, shifts = transforms(steps * blocks)
    same = np.eye(4).reshape(4, 2, 2)
    forward = forward.reshape(blocks, steps * 2, 2, LANES // 2)
    forward = np.einsum("itks,chp->tcipkhs", forward, same).reshape(4 * LANES, 4 * LANES)
    inverse = inverse.reshape(2, LANES // 2, blocks, steps * 2)
    inverse = np.einsum("ksit,chp->pkhstci", inverse, same).reshape(4 * LANES, 4 * LANES)
    forward_high, forward_low = split_const(forward)
    inverse_high, inverse_low = split_const(inverse)

    edges = tiles * planes * (2 * steps + 1) + planes * rows
    to_down, to_up, last, first = call(
        functools.partial(pack_kernel, own_cols),
        [f32(edges, LANES), f32(edges, LANES), f32(planes, rows, cols), f32(planes, rows, cols)],
        [v32(*state.shape), v32(*state.shape), v32(*conductivity.shape), pltpu.SemaphoreType.DMA((3,))],
        10**5,
        10**6,
        me.reshape(1), state, adjoint, conductivity,
        places="shhh",
        limit=WHOLE_VMEM,
    )
    top = shift(to_down, "space", 1)
    bottom = shift(to_up, "space", -1)
    prior = shift(last, "tm", 1)
    later = shift(first, "tm", -1)
    partial = call(
        local_kernel,
        f32(LANES, cols),
        [v32(*state.shape)] * 4 + [v32(*conductivity.shape), pltpu.SemaphoreType.DMA((5,))],
        10**7,
        3 * 10**6,
        state, adjoint, source, target, conductivity,
        places="hhhhh",
        limit=WHOLE_VMEM,
    )
    place = lax.axis_index("space")
    sent = call(
        functools.partial(finish_kernel, (blocks, steps, planes, rows, (0, lax.axis_size("space") - 1))),
        f32(blocks, span, LANES),
        [v32(LANES, cols), v32(cols + 2 * WIDE, LANES)],
        10**7,
        3 * 10**6,
        place.reshape(1), partial, to_down, to_up, prior, later, top, bottom,
        places="s",
    )
    got = lax.all_to_all(sent, "tm", 0, 0, tiled=True).reshape(blocks * span, LANES)
    own, up, down = call(
        functools.partial(forward_kernel, (blocks, span, planes, rows)),
        [f32(rows * line, LANES), f32(DEEP * line, LANES), f32(DEEP * line, LANES)],
        [
            v32(span // 4 * planes * rows, 4 * LANES),
            pltpu.VMEM(forward_high.shape, jnp.bfloat16),
            pltpu.VMEM(forward_low.shape, jnp.bfloat16),
            pltpu.SemaphoreType.DMA((2,)),
        ],
        6 * 10**8,
        4 * 10**6,
        got, forward_high, forward_low,
        places="vhh",
    )
    above = shift(down, "space", 1)
    below = shift(up, "space", -1)

    def unpack(packed, end):
        rim = packed[edges - planes * rows :].reshape(planes, rows, LANES)[..., :span]
        return jnp.where(place == end, 0.0, rim)

    kappa = jnp.concatenate([unpack(top, 0), unpack(to_up, -1), unpack(bottom, lax.axis_size("space") - 1)], axis=1)
    kappa = jnp.stack([kappa[..., : span // 2], kappa[..., : span // 2 - 1 : -1]], axis=2)
    kappa = kappa.reshape(planes, 3 * rows, 2, SUBLANES, strip).transpose(1, 3, 2, 0, 4).reshape(3 * rows, SUBLANES, 2 * count)
    kappa = jnp.pad(kappa, ((0, 0), (0, 0), (0, LANES - 2 * count)))
    weights = call(
        functools.partial(weight_kernel, (planes, strip)),
        [
            f32(tall, count, *tile),
            f32(tall, planes * (strip + 1), *tile),
            f32(tall, count - strip, *tile),
            f32(tall, count, *tile),
            f32(tall, count, *tile),
        ],
        [v32(3 * rows, count, *tile)],
        10**9,
        10**7,
        kappa, np.tile(shifts.reshape(2, 2, -1)[:, :1], (1, 2, 1)).reshape(2, LANES),
    )
    back = call(
        functools.partial(sweep_kernel, (blocks, own_cols, planes, strip)),
        f32(blocks * own_cols, LANES),
        [
            v32(tall, 2 * count, *tile),
            v32(tall * line, LANES),
            v32(tall * line, LANES),
            v32(own_cols // 4 * planes * rows, 4 * LANES),
        ],
        10**9,
        6 * 10**6,
        own.reshape(rows, 2 * count, *tile), above.reshape(DEEP, 2 * count, *tile), below.reshape(DEEP, 2 * count, *tile),
        *weights, inverse_high, inverse_low,
    )
    got_back = lax.all_to_all(back, "tm", 0, 0, tiled=True)
    return tuple(
        call(update_kernel, [f32(*state.shape), f32(*state.shape)], [], 10**6, 2 * 10**6, got_back, state, adjoint)
    )


def solution(mesh):
    split = P("tm", None, "space", None)
    return jax.shard_map(
        body,
        mesh=mesh,
        in_specs=(split, split, split, split, P(None, "space", None)),
        out_specs=(split, split),
        check_vma=False,
    )
```

```python
import functools
import math

import jax
import jax.numpy as jnp
import ml_dtypes
import numpy as np
from jax import lax
from jax.experimental import pallas as pl
from jax.experimental.pallas import tpu as pltpu
from jax.sharding import PartitionSpec as P

SWEEPS = 8
STEP = 0.5
PENALTY = 0.05
LANES = 128
WIDE = 8
DEEP = SWEEPS - 1
SUBLANES = 8
VMEM_LIMIT = 28 * 1024 * 1024
WHOLE_VMEM = 60 * 1024 * 1024
PACK_VMEM = 54682 * 1024


def transforms(period):
    q = STEP / PENALTY
    time = np.arange(period)
    pairs = [(0, 1)] + [(k, s) for k in range(1, period // 2) for s in (1, -1)] + [(period // 2, 1)]
    count = len(pairs)
    forward = np.zeros((period, 2, 2 * count))
    inverse = np.zeros((2 * count, period, 2))
    real_shift, imag_shift = np.zeros(count), np.zeros(count)
    for m, (k, sign) in enumerate(pairs):
        theta = 2.0 * math.pi * k / period
        sine = 0.0 if k in (0, period // 2) else math.sin(theta)
        root = math.sqrt(sine * sine + STEP * q)
        real_shift[m] = 1.0 - math.cos(theta)
        imag_shift[m] = sign * root
        wave = np.exp(-1j * theta * time)
        first = (root + sign * sine) / (2.0 * q * root) * wave
        second = -sign * 1j / (2.0 * root) * wave
        for f, row in enumerate((first, second)):
            forward[:, f, m] = row.real
            forward[:, f, count + m] = row.imag
        weight = 2.0 / period
        back = np.conj(wave) * weight
        for f, factor in enumerate((q, sign * 1j * (root - sign * sine))):
            inverse[m, :, f] = (factor * back).real
            inverse[count + m, :, f] = -(factor * back).imag
    real_lane = np.concatenate([real_shift, real_shift])
    imag_lane = np.concatenate([imag_shift, -imag_shift])
    return forward, inverse, np.stack([real_lane, imag_lane]).astype(np.float32)


def split_const(matrix):
    high = matrix.astype(np.float32).astype(ml_dtypes.bfloat16)
    low = (matrix - high.astype(np.float64)).astype(np.float32).astype(ml_dtypes.bfloat16)
    return high, low


def dot_split(left, high_ref, low_ref):
    high = left.astype(jnp.bfloat16)
    low = (left - high.astype(jnp.float32)).astype(jnp.bfloat16)
    dot = functools.partial(jnp.dot, preferred_element_type=jnp.float32)
    return dot(high, high_ref[...]) + (dot(low, high_ref[...]) + dot(high, low_ref[...]))


def fetch(sources, targets, sems):
    copies = [pltpu.make_async_copy(x, y, sems.at[i]) for i, (x, y) in enumerate(zip(sources, targets))]
    for copy in copies:
        copy.start()
    return copies


def pack_kernel(own_cols, me, state_far, adjoint_far, cond_far, to_down, to_up, last, first, state, adjoint, cond, sems):
    steps, planes, rows, cols = state.shape
    tiles = cols // LANES
    per_tile = 2 * steps * planes
    for copy in fetch((state_far, adjoint_far, cond_far), (state, adjoint, cond), sems):
        copy.wait()
    for out, r in ((to_down, rows - 1), (to_up, 0)):
        for k in range(tiles):
            lanes = pl.ds(k * LANES, LANES)
            for f, field in enumerate((state, adjoint)):
                for t in range(steps):
                    for p in range(planes):
                        out[pl.ds(k * per_tile + (f * steps + t) * planes + p, 1), :] = field[t, p, pl.ds(r, 1), lanes]
            for p in range(planes):
                out[pl.ds(tiles * per_tile + k * planes + p, 1), :] = cond[p, pl.ds(r, 1), lanes]
    start = me[0] * own_cols - WIDE
    column = lax.broadcasted_iota(jnp.int32, (rows, LANES), 1) + start
    base = tiles * (per_tile + planes)
    for p in range(planes):
        turned = pltpu.roll(cond[p], lax.rem(cols - start, cols), axis=1)[:, :LANES]
        slab = jnp.where((column >= 0) & (column < cols), turned, 0.0)
        to_down[pl.ds(base + p * rows, rows), :] = slab
        to_up[pl.ds(base + p * rows, rows), :] = slab
    last[...] = state[steps - 1]
    first[...] = adjoint[0]


def edge_row(packed, tiles, base, stride, at):
    return jnp.concatenate([packed[pl.ds(base + k * stride + at, 1), :] for k in range(tiles)], axis=1)


def local_kernel(*refs):
    count = 5
    out, sems = refs[count], refs[-1]
    state, adjoint, source, target, cond = refs[count + 1 : 2 * count + 1]
    for copy in fetch(refs[:count], refs[count + 1 : 2 * count + 1], sems):
        copy.wait()
    steps, planes, rows, cols = state.shape
    row = lax.broadcasted_iota(jnp.int32, (rows, cols), 0)
    col = lax.broadcasted_iota(jnp.int32, (rows, cols), 1)

    def near(value):
        return (
            pltpu.roll(value, 1, axis=0),
            pltpu.roll(value, rows - 1, axis=0),
            jnp.where(col == 0, 0.0, pltpu.roll(value, 1, axis=1)),
            jnp.where(col == cols - 1, 0.0, pltpu.roll(value, cols - 1, axis=1)),
        )

    kappa = [cond[p] for p in range(planes)]
    zero = jnp.zeros((rows, cols), jnp.float32)
    for p in range(planes):
        around = near(kappa[p])
        around += (kappa[p - 1] if p else zero, kappa[p + 1] if p < planes - 1 else zero)
        weights = [(0.5 * STEP) * (kappa[p] + k) for k in around]
        weights[0] = jnp.where(row == 0, 0.0, weights[0])
        weights[1] = jnp.where(row == rows - 1, 0.0, weights[1])
        diag = weights[0]
        for w in weights[1:]:
            diag = diag + w
        for t in range(steps):
            stiff = []
            for field in (state, adjoint):
                value = field[t, p]
                total = diag * value
                for w, v in zip(weights, near(value)):
                    total = total - w * v
                if p:
                    total = total - weights[4] * field[t, p - 1]
                if p < planes - 1:
                    total = total - weights[5] * field[t, p + 1]
                stiff.append(total)
            s, a = state[t, p], adjoint[t, p]
            s_step = s - state[t - 1, p] if t else s
            a_step = a - adjoint[t + 1, p] if t < steps - 1 else a
            first = STEP * source[t, p] - (s_step + stiff[0] + (STEP / PENALTY) * a)
            second = -STEP * target[t, p] - (a_step + stiff[1] - STEP * s)
            for f, value in enumerate((first, second)):
                out[pl.ds(((t * 2 + f) * planes + p) * rows, rows), :] = value


def finish_kernel(shape, place, partial, to_down, to_up, prior, later, top, bottom, out, res, turned):
    blocks, steps, planes, rows, ends = shape
    cols = partial.shape[1]
    tiles = cols // LANES
    per_tile = 2 * steps * planes
    row = lax.broadcasted_iota(jnp.int32, (rows, cols), 0)
    inside = [jnp.where(place[0] == end, 0.0, 1.0) for end in ends]
    sides = ((0, to_up, top), (rows - 1, to_down, bottom))
    for p in range(planes):
        weights = []
        for i, (_, mine, other) in enumerate(sides):
            here = edge_row(mine, tiles, tiles * per_tile, planes, p)
            beyond = edge_row(other, tiles, tiles * per_tile, planes, p)
            weights.append((0.5 * STEP) * (here + beyond * inside[i]))
        for t in range(steps):
            for f in range(2):
                at = ((t * 2 + f) * planes + p) * rows
                edge = (f * steps + t) * planes + p
                total = partial[pl.ds(at, rows), :]
                for i, (r, mine, other) in enumerate(sides):
                    here = edge_row(mine, tiles, 0, per_tile, edge)
                    beyond = edge_row(other, tiles, 0, per_tile, edge)
                    total = jnp.where(row == r, total - weights[i] * (here - beyond * inside[i]), total)
                if f == 0 and t == 0:
                    total = total + prior[p]
                if f == 1 and t == steps - 1:
                    total = total + later[p]
                res[pl.ds(at, rows), :] = total
    turned[pl.ds(0, WIDE), :] = jnp.zeros((WIDE, LANES), jnp.float32)
    turned[pl.ds(WIDE + cols, WIDE), :] = jnp.zeros((WIDE, LANES), jnp.float32)
    for tile in range(tiles):
        turned[pl.ds(WIDE + tile * LANES, LANES), :] = res[:, pl.ds(tile * LANES, LANES)].T
    own = cols // blocks
    for j in range(blocks):
        out[j] = turned[pl.ds(j * own, own + 2 * WIDE), :]


def column_group(g, span):
    near = [2 * g, 2 * g + 1]
    return near + [span - 1 - c for c in near]


def forward_kernel(shape, got, high_far, low_far, own, up, down, left, high, low, sems):
    blocks, span, planes, rows = shape
    copies = fetch((high_far, low_far), (high, low), sems)
    strip = span // (2 * SUBLANES)
    line = planes * span
    cells = planes * rows
    for g in range(span // 4):
        parts = [got[pl.ds(c, blocks, stride=span), :] for c in column_group(g, span)]
        turned = jnp.concatenate(parts, axis=0).T
        for tf in range(4):
            left[pl.ds(g * cells, cells), pl.ds(tf * LANES, LANES)] = turned[tf * cells : (tf + 1) * cells]
    for copy in copies:
        copy.wait()
    spectrum = dot_split(left[...], high, low)
    for g in range(span // 4):
        for pair in range(2):
            sub, at = divmod(2 * g + pair, strip)
            for part in range(2):
                lane = (2 * pair + part) * LANES
                for p in range(planes):
                    piece = spectrum[g * cells + p * rows : g * cells + (p + 1) * rows, lane : lane + LANES]
                    begin = ((p * strip + at) * 2 + part) * SUBLANES + sub
                    own[pl.ds(begin, rows, stride=line), :] = piece
    up[...] = own[pl.ds(0, line * DEEP), :]
    down[...] = own[pl.ds(line, line * DEEP), :]


def weight_kernel(shape, kappa, shifts, w_row, w_col, w_plane, scale, cross, wide):
    planes, strip = shape
    count = planes * strip
    tall = scale.shape[0]
    sub = lax.broadcasted_iota(jnp.int32, (SUBLANES, LANES), 0)
    mirrored = lax.broadcasted_iota(jnp.int32, (SUBLANES, LANES), 1) >= LANES // 2
    real = jnp.broadcast_to(shifts[0:1, :], (SUBLANES, LANES))
    imag = jnp.broadcast_to(shifts[1:2, :], (SUBLANES, LANES))

    def spread(r, _):
        packed = kappa[r]
        for n in range(count):
            a = jnp.broadcast_to(packed[:, n : n + 1], (SUBLANES, LANES))
            b = jnp.broadcast_to(packed[:, count + n : count + n + 1], (SUBLANES, LANES))
            wide[r, n] = jnp.where(mirrored, b, a)

    def bond(a, b):
        return jnp.where(a * b > 0.0, (0.5 * STEP) * (a + b), 0.0)

    def setup(r, _):
        here = [wide[r + 1, n] for n in range(count)]
        for p in range(planes):
            for c in range(strip):
                n = p * strip + c
                mine = here[n]
                if c:
                    to_left = here[n - 1]
                else:
                    to_left = jnp.where(sub == 0, 0.0, pltpu.roll(here[n + strip - 1], 1, axis=0))
                    w_col[r, p * (strip + 1)] = bond(mine, to_left)
                if c < strip - 1:
                    to_right = here[n + 1]
                else:
                    to_right = pltpu.roll(here[n - strip + 1], SUBLANES - 1, axis=0)
                    to_right = jnp.where(sub == SUBLANES - 1, pltpu.roll(mine, LANES // 2, axis=1), to_right)
                w_col[r, p * (strip + 1) + c + 1] = bond(mine, to_right)
                below = wide[r + 2, n]
                w_row[r, n] = bond(mine, below)
                around = wide[r, n] + below + to_left + to_right
                if p:
                    around = around + here[n - strip]
                if p < planes - 1:
                    around = around + here[n + strip]
                    w_plane[r, n] = bond(mine, here[n + strip])
                big = (0.5 * STEP) * (6.0 * mine + around) + real
                inv = 1.0 / (big * big + imag * imag)
                scale[r, n] = big * inv
                cross[r, n] = imag * inv

    lax.fori_loop(0, tall + 2, spread, None)
    lax.fori_loop(0, tall, setup, None)


def sweep_kernel(shape, own, above, below, w_row, w_col, w_plane, scale, cross, high, low, out, rhs, first, second, left):
    blocks, own_cols, planes, strip = shape
    rows = own.shape[0]
    tall = rows + 2 * DEEP
    count = planes * strip
    line = 2 * count * SUBLANES
    sub = lax.broadcasted_iota(jnp.int32, (SUBLANES, LANES), 0)

    def at(r, n):
        return pl.ds(pl.multiple_of((r * 2 * count + n) * SUBLANES, SUBLANES), SUBLANES)

    def solve(target, totals, r, m):
        a, b = scale[r, m], cross[r, m]
        target[at(r, 2 * m), :] = a * totals[0] + b * totals[1]
        target[at(r, 2 * m + 1), :] = a * totals[1] - b * totals[0]

    for source, offset in ((above, 0), (own, DEEP), (below, DEEP + rows)):

        def start(r, _, source=source, offset=offset):
            for m in range(count):
                pair = [source[r, 2 * m + k] for k in range(2)]
                for k in range(2):
                    rhs[r + offset, 2 * m + k] = pair[k]
                solve(first, pair, r + offset, m)

        lax.fori_loop(0, source.shape[0], start, None)

    def relax(old, new, r):
        here = [[old[at(r, 2 * m + k), :] for k in range(2)] for m in range(count)]
        for p in range(planes):
            base = p * strip
            before = [pltpu.roll(v, 1, axis=0) for v in here[base + strip - 1]]
            across = [pltpu.roll(v, LANES // 2, axis=1) for v in here[base + strip - 1]]
            after = [pltpu.roll(v, SUBLANES - 1, axis=0) for v in here[base]]
            after = [jnp.where(sub == SUBLANES - 1, x, v) for x, v in zip(across, after)]
            for c in range(strip):
                m = base + c
                flank = p * (strip + 1) + c
                totals = []
                for k in range(2):
                    to_left = here[m - 1][k] if c else before[k]
                    to_right = here[m + 1][k] if c < strip - 1 else after[k]
                    total = w_col[r, flank] * to_left + w_col[r, flank + 1] * to_right
                    others = w_row[r, m] * old[at(r + 1, 2 * m + k), :] + w_row[r - 1, m] * old[at(r - 1, 2 * m + k), :]
                    mine = rhs[r, 2 * m + k]
                    if p:
                        mine = mine + w_plane[r, m - strip] * here[m - strip][k]
                    if p < planes - 1:
                        others = others + w_plane[r, m] * here[m + strip][k]
                    totals.append(mine + (total + others))
                solve(new, totals, r, m)

    old, new = first, second
    for sweep in range(1, SWEEPS):

        def step(q, _, old=old, new=new, sweep=sweep):
            relax(old, new, sweep + 2 * q)
            relax(old, new, sweep + 2 * q + 1)

        lax.fori_loop(0, (tall - 2 * sweep) // 2, step, None)
        old, new = new, old

    cells = planes * rows
    for g in range(own_cols // 4):
        for pair in range(2):
            side, place = divmod(2 * g + pair + WIDE, strip)
            for part in range(2):
                for p in range(planes):
                    begin = DEEP * line + ((p * strip + place) * 2 + part) * SUBLANES + side
                    piece = old[pl.ds(begin, rows, stride=line), :]
                    left[pl.ds(g * cells + p * rows, rows), pl.ds((2 * pair + part) * LANES, LANES)] = piece
    values = dot_split(left[...], high, low)
    for g in range(own_cols // 4):
        parts = [values[g * cells : (g + 1) * cells, tf * LANES : (tf + 1) * LANES] for tf in range(4)]
        turned = jnp.concatenate(parts, axis=0).T
        for c, column in enumerate(column_group(g, own_cols)):
            out[pl.ds(column, blocks, stride=own_cols), :] = turned[c * blocks : (c + 1) * blocks]


def update_kernel(got, state, adjoint, new_state, new_adjoint):
    steps, planes, rows, cols = state.shape
    for tile in range(cols // LANES):
        block = got[pl.ds(tile * LANES, LANES), :].T
        for t in range(steps):
            for f, (old, new) in enumerate(((state, new_state), (adjoint, new_adjoint))):
                for p in range(planes):
                    at = ((t * 2 + f) * planes + p) * rows
                    new[t, p, :, pl.ds(tile * LANES, LANES)] = (
                        old[t, p, :, pl.ds(tile * LANES, LANES)] + block[at : at + rows]
                    )


def call(kernel, outs, scratch, flops, moved, *args, places="", limit=VMEM_LIMIT):
    spaces = {"s": pltpu.SMEM, "h": pltpu.HBM, "v": pltpu.VMEM}
    vmem = pl.BlockSpec(memory_space=pltpu.VMEM)
    return pl.pallas_call(
        kernel,
        out_shape=outs,
        in_specs=[pl.BlockSpec(memory_space=spaces[x]) for x in places.ljust(len(args), "v")],
        out_specs=[vmem] * len(outs) if isinstance(outs, list) else vmem,
        scratch_shapes=scratch,
        compiler_params=pltpu.CompilerParams(vmem_limit_bytes=limit),
        cost_estimate=pl.CostEstimate(flops=flops, bytes_accessed=moved, transcendentals=0),
    )(*args)


def v32(*shape):
    return pltpu.VMEM(shape, jnp.float32)


def f32(*shape):
    return jax.ShapeDtypeStruct(shape, jnp.float32)


def shift(block, axis, distance):
    count = lax.axis_size(axis)
    return lax.ppermute(block, axis, [(i, (i + distance) % count) for i in range(count)])


def body(state, adjoint, source, target, conductivity):
    steps, planes, rows, cols = state.shape
    blocks = lax.axis_size("tm")
    me = lax.axis_index("tm")
    own_cols = cols // blocks
    span = own_cols + 2 * WIDE
    strip = span // (2 * SUBLANES)
    count = planes * strip
    line = 2 * count * SUBLANES
    tall = rows + 2 * DEEP
    tiles = cols // LANES
    tile = (SUBLANES, LANES)

    forward, inverse, shifts = transforms(steps * blocks)
    same = np.eye(4).reshape(4, 2, 2)
    forward = forward.reshape(blocks, steps * 2, 2, LANES // 2)
    forward = np.einsum("itks,chp->tcipkhs", forward, same).reshape(4 * LANES, 4 * LANES)
    inverse = inverse.reshape(2, LANES // 2, blocks, steps * 2)
    inverse = np.einsum("ksit,chp->pkhstci", inverse, same).reshape(4 * LANES, 4 * LANES)
    forward_high, forward_low = split_const(forward)
    inverse_high, inverse_low = split_const(inverse)

    edges = tiles * planes * (2 * steps + 1) + planes * rows
    to_down, to_up, last, first = call(
        functools.partial(pack_kernel, own_cols),
        [f32(edges, LANES), f32(edges, LANES), f32(planes, rows, cols), f32(planes, rows, cols)],
        [v32(*state.shape), v32(*state.shape), v32(*conductivity.shape), pltpu.SemaphoreType.DMA((3,))],
        10**5,
        10**6,
        me.reshape(1), state, adjoint, conductivity,
        places="shhh",
        limit=PACK_VMEM,
    )
    top = shift(to_down, "space", 1)
    bottom = shift(to_up, "space", -1)
    prior = shift(last, "tm", 1)
    later = shift(first, "tm", -1)
    partial = call(
        local_kernel,
        f32(LANES, cols),
        [v32(*state.shape)] * 4 + [v32(*conductivity.shape), pltpu.SemaphoreType.DMA((5,))],
        10**7,
        3 * 10**6,
        state, adjoint, source, target, conductivity,
        places="hhhhh",
        limit=WHOLE_VMEM,
    )
    place = lax.axis_index("space")
    sent = call(
        functools.partial(finish_kernel, (blocks, steps, planes, rows, (0, lax.axis_size("space") - 1))),
        f32(blocks, span, LANES),
        [v32(LANES, cols), v32(cols + 2 * WIDE, LANES)],
        10**7,
        3 * 10**6,
        place.reshape(1), partial, to_down, to_up, prior, later, top, bottom,
        places="s",
    )
    got = lax.all_to_all(sent, "tm", 0, 0, tiled=True).reshape(blocks * span, LANES)
    own, up, down = call(
        functools.partial(forward_kernel, (blocks, span, planes, rows)),
        [f32(rows * line, LANES), f32(DEEP * line, LANES), f32(DEEP * line, LANES)],
        [
            v32(span // 4 * planes * rows, 4 * LANES),
            pltpu.VMEM(forward_high.shape, jnp.bfloat16),
            pltpu.VMEM(forward_low.shape, jnp.bfloat16),
            pltpu.SemaphoreType.DMA((2,)),
        ],
        6 * 10**8,
        4 * 10**6,
        got, forward_high, forward_low,
        places="vhh",
    )
    above = shift(down, "space", 1)
    below = shift(up, "space", -1)

    def unpack(packed, end):
        rim = packed[edges - planes * rows :].reshape(planes, rows, LANES)[..., :span]
        return jnp.where(place == end, 0.0, rim)

    kappa = jnp.concatenate([unpack(top, 0), unpack(to_up, -1), unpack(bottom, lax.axis_size("space") - 1)], axis=1)
    kappa = jnp.stack([kappa[..., : span // 2], kappa[..., : span // 2 - 1 : -1]], axis=2)
    kappa = kappa.reshape(planes, 3 * rows, 2, SUBLANES, strip).transpose(1, 3, 2, 0, 4).reshape(3 * rows, SUBLANES, 2 * count)
    kappa = jnp.pad(kappa, ((0, 0), (0, 0), (0, LANES - 2 * count)))
    weights = call(
        functools.partial(weight_kernel, (planes, strip)),
        [
            f32(tall, count, *tile),
            f32(tall, planes * (strip + 1), *tile),
            f32(tall, count - strip, *tile),
            f32(tall, count, *tile),
            f32(tall, count, *tile),
        ],
        [v32(3 * rows, count, *tile)],
        10**9,
        10**7,
        kappa, np.tile(shifts.reshape(2, 2, -1)[:, :1], (1, 2, 1)).reshape(2, LANES),
    )
    back = call(
        functools.partial(sweep_kernel, (blocks, own_cols, planes, strip)),
        f32(blocks * own_cols, LANES),
        [
            v32(tall, 2 * count, *tile),
            v32(tall * line, LANES),
            v32(tall * line, LANES),
            v32(own_cols // 4 * planes * rows, 4 * LANES),
        ],
        10**9,
        6 * 10**6,
        own.reshape(rows, 2 * count, *tile), above.reshape(DEEP, 2 * count, *tile), below.reshape(DEEP, 2 * count, *tile),
        *weights, inverse_high, inverse_low,
    )
    got_back = lax.all_to_all(back, "tm", 0, 0, tiled=True)
    return tuple(
        call(update_kernel, [f32(*state.shape), f32(*state.shape)], [], 10**6, 2 * 10**6, got_back, state, adjoint)
    )


def solution(mesh):
    split = P("tm", None, "space", None)
    return jax.shard_map(
        body,
        mesh=mesh,
        in_specs=(split, split, split, split, P(None, "space", None)),
        out_specs=(split, split),
        check_vma=False,
    )
```

```python
import functools
import math

import jax
import jax.numpy as jnp
import ml_dtypes
import numpy as np
from jax import lax
from jax.experimental import pallas as pl
from jax.experimental.pallas import tpu as pltpu
from jax.sharding import PartitionSpec as P

SWEEPS = 8
STEP = 0.5
PENALTY = 0.05
LANES = 128
WIDE = 8
DEEP = SWEEPS - 1
SUBLANES = 8
VMEM_LIMIT = 28 * 1024 * 1024
WHOLE_VMEM = 60 * 1024 * 1024
PACK_VMEM = 54682 * 1024


def transforms(period):
    q = STEP / PENALTY
    time = np.arange(period)
    pairs = [(0, 1)] + [(k, s) for k in range(1, period // 2) for s in (1, -1)] + [(period // 2, 1)]
    count = len(pairs)
    forward = np.zeros((period, 2, 2 * count))
    inverse = np.zeros((2 * count, period, 2))
    real_shift, imag_shift = np.zeros(count), np.zeros(count)
    for m, (k, sign) in enumerate(pairs):
        theta = 2.0 * math.pi * k / period
        sine = 0.0 if k in (0, period // 2) else math.sin(theta)
        root = math.sqrt(sine * sine + STEP * q)
        real_shift[m] = 1.0 - math.cos(theta)
        imag_shift[m] = sign * root
        wave = np.exp(-1j * theta * time)
        first = (root + sign * sine) / (2.0 * q * root) * wave
        second = -sign * 1j / (2.0 * root) * wave
        for f, row in enumerate((first, second)):
            forward[:, f, m] = row.real
            forward[:, f, count + m] = row.imag
        weight = 2.0 / period
        back = np.conj(wave) * weight
        for f, factor in enumerate((q, sign * 1j * (root - sign * sine))):
            inverse[m, :, f] = (factor * back).real
            inverse[count + m, :, f] = -(factor * back).imag
    real_lane = np.concatenate([real_shift, real_shift])
    imag_lane = np.concatenate([imag_shift, -imag_shift])
    return forward, inverse, np.stack([real_lane, imag_lane]).astype(np.float32)


def split_const(matrix):
    high = matrix.astype(np.float32).astype(ml_dtypes.bfloat16)
    low = (matrix - high.astype(np.float64)).astype(np.float32).astype(ml_dtypes.bfloat16)
    return high, low


def dot_split(left, high_ref, low_ref):
    high = left.astype(jnp.bfloat16)
    low = (left - high.astype(jnp.float32)).astype(jnp.bfloat16)
    dot = functools.partial(jnp.dot, preferred_element_type=jnp.float32)
    return dot(high, high_ref[...]) + (dot(low, high_ref[...]) + dot(high, low_ref[...]))


def fetch(sources, targets, sems):
    copies = [pltpu.make_async_copy(x, y, sems.at[i]) for i, (x, y) in enumerate(zip(sources, targets))]
    for copy in copies:
        copy.start()
    return copies


def pack_kernel(own_cols, me, state_far, adjoint_far, cond_far, to_down, to_up, last, first, state, adjoint, cond, sems):
    steps, planes, rows, cols = state.shape
    tiles = cols // LANES
    per_tile = 2 * steps * planes
    for copy in fetch((state_far, adjoint_far, cond_far), (state, adjoint, cond), sems):
        copy.wait()
    for out, r in ((to_down, rows - 1), (to_up, 0)):
        for k in range(tiles):
            lanes = pl.ds(k * LANES, LANES)
            for f, field in enumerate((state, adjoint)):
                for t in range(steps):
                    for p in range(planes):
                        out[pl.ds(k * per_tile + (f * steps + t) * planes + p, 1), :] = field[t, p, pl.ds(r, 1), lanes]
            for p in range(planes):
                out[pl.ds(tiles * per_tile + k * planes + p, 1), :] = cond[p, pl.ds(r, 1), lanes]
    start = me[0] * own_cols - WIDE
    column = lax.broadcasted_iota(jnp.int32, (rows, LANES), 1) + start
    base = tiles * (per_tile + planes)
    for p in range(planes):
        turned = pltpu.roll(cond[p], lax.rem(cols - start, cols), axis=1)[:, :LANES]
        slab = jnp.where((column >= 0) & (column < cols), turned, 0.0)
        to_down[pl.ds(base + p * rows, rows), :] = slab
        to_up[pl.ds(base + p * rows, rows), :] = slab
    last[...] = state[steps - 1]
    first[...] = adjoint[0]


def edge_row(packed, tiles, base, stride, at):
    return jnp.concatenate([packed[pl.ds(base + k * stride + at, 1), :] for k in range(tiles)], axis=1)


def local_kernel(*refs):
    count = 5
    out, sems = refs[count], refs[-1]
    state, adjoint, source, target, cond = refs[count + 1 : 2 * count + 1]
    for copy in fetch(refs[:count], refs[count + 1 : 2 * count + 1], sems):
        copy.wait()
    steps, planes, rows, cols = state.shape
    row = lax.broadcasted_iota(jnp.int32, (rows, cols), 0)
    col = lax.broadcasted_iota(jnp.int32, (rows, cols), 1)

    def near(value):
        return (
            pltpu.roll(value, 1, axis=0),
            pltpu.roll(value, rows - 1, axis=0),
            jnp.where(col == 0, 0.0, pltpu.roll(value, 1, axis=1)),
            jnp.where(col == cols - 1, 0.0, pltpu.roll(value, cols - 1, axis=1)),
        )

    kappa = [cond[p] for p in range(planes)]
    zero = jnp.zeros((rows, cols), jnp.float32)
    for p in range(planes):
        around = near(kappa[p])
        around += (kappa[p - 1] if p else zero, kappa[p + 1] if p < planes - 1 else zero)
        weights = [(0.5 * STEP) * (kappa[p] + k) for k in around]
        weights[0] = jnp.where(row == 0, 0.0, weights[0])
        weights[1] = jnp.where(row == rows - 1, 0.0, weights[1])
        diag = weights[0]
        for w in weights[1:]:
            diag = diag + w
        for t in range(steps):
            stiff = []
            for field in (state, adjoint):
                value = field[t, p]
                total = diag * value
                for w, v in zip(weights, near(value)):
                    total = total - w * v
                if p:
                    total = total - weights[4] * field[t, p - 1]
                if p < planes - 1:
                    total = total - weights[5] * field[t, p + 1]
                stiff.append(total)
            s, a = state[t, p], adjoint[t, p]
            s_step = s - state[t - 1, p] if t else s
            a_step = a - adjoint[t + 1, p] if t < steps - 1 else a
            first = STEP * source[t, p] - (s_step + stiff[0] + (STEP / PENALTY) * a)
            second = -STEP * target[t, p] - (a_step + stiff[1] - STEP * s)
            for f, value in enumerate((first, second)):
                out[pl.ds(((t * 2 + f) * planes + p) * rows, rows), :] = value


def finish_kernel(shape, place, partial, to_down, to_up, prior, later, top, bottom, out, res, turned):
    blocks, steps, planes, rows, ends = shape
    cols = partial.shape[1]
    tiles = cols // LANES
    per_tile = 2 * steps * planes
    row = lax.broadcasted_iota(jnp.int32, (rows, cols), 0)
    inside = [jnp.where(place[0] == end, 0.0, 1.0) for end in ends]
    sides = ((0, to_up, top), (rows - 1, to_down, bottom))
    for p in range(planes):
        weights = []
        for i, (_, mine, other) in enumerate(sides):
            here = edge_row(mine, tiles, tiles * per_tile, planes, p)
            beyond = edge_row(other, tiles, tiles * per_tile, planes, p)
            weights.append((0.5 * STEP) * (here + beyond * inside[i]))
        for t in range(steps):
            for f in range(2):
                at = ((t * 2 + f) * planes + p) * rows
                edge = (f * steps + t) * planes + p
                total = partial[pl.ds(at, rows), :]
                for i, (r, mine, other) in enumerate(sides):
                    here = edge_row(mine, tiles, 0, per_tile, edge)
                    beyond = edge_row(other, tiles, 0, per_tile, edge)
                    total = jnp.where(row == r, total - weights[i] * (here - beyond * inside[i]), total)
                if f == 0 and t == 0:
                    total = total + prior[p]
                if f == 1 and t == steps - 1:
                    total = total + later[p]
                res[pl.ds(at, rows), :] = total
    turned[pl.ds(0, WIDE), :] = jnp.zeros((WIDE, LANES), jnp.float32)
    turned[pl.ds(WIDE + cols, WIDE), :] = jnp.zeros((WIDE, LANES), jnp.float32)
    for tile in range(tiles):
        turned[pl.ds(WIDE + tile * LANES, LANES), :] = res[:, pl.ds(tile * LANES, LANES)].T
    own = cols // blocks
    for j in range(blocks):
        out[j] = turned[pl.ds(j * own, own + 2 * WIDE), :]


def column_group(g, span):
    near = [2 * g, 2 * g + 1]
    return near + [span - 1 - c for c in near]


def forward_kernel(shape, got, high_far, low_far, own, up, down, left, high, low, sems):
    blocks, span, planes, rows = shape
    copies = fetch((high_far, low_far), (high, low), sems)
    strip = span // (2 * SUBLANES)
    line = planes * span
    cells = planes * rows
    for g in range(span // 4):
        parts = [got[pl.ds(c, blocks, stride=span), :] for c in column_group(g, span)]
        turned = jnp.concatenate(parts, axis=0).T
        for tf in range(4):
            left[pl.ds(g * cells, cells), pl.ds(tf * LANES, LANES)] = turned[tf * cells : (tf + 1) * cells]
    for copy in copies:
        copy.wait()
    spectrum = dot_split(left[...], high, low)
    for g in range(span // 4):
        for pair in range(2):
            sub, at = divmod(2 * g + pair, strip)
            for part in range(2):
                lane = (2 * pair + part) * LANES
                for p in range(planes):
                    piece = spectrum[g * cells + p * rows : g * cells + (p + 1) * rows, lane : lane + LANES]
                    begin = ((p * strip + at) * 2 + part) * SUBLANES + sub
                    own[pl.ds(begin, rows, stride=line), :] = piece
    up[...] = own[pl.ds(0, line * DEEP), :]
    down[...] = own[pl.ds(line, line * DEEP), :]


def weight_kernel(shape, kappa, shifts, w_row, w_col, w_plane, scale, cross, wide):
    planes, strip = shape
    count = planes * strip
    tall = scale.shape[0]
    sub = lax.broadcasted_iota(jnp.int32, (SUBLANES, LANES), 0)
    mirrored = lax.broadcasted_iota(jnp.int32, (SUBLANES, LANES), 1) >= LANES // 2
    real = jnp.broadcast_to(shifts[0:1, :], (SUBLANES, LANES))
    imag = jnp.broadcast_to(shifts[1:2, :], (SUBLANES, LANES))

    def spread(r, _):
        packed = kappa[r]
        for n in range(count):
            a = jnp.broadcast_to(packed[:, n : n + 1], (SUBLANES, LANES))
            b = jnp.broadcast_to(packed[:, count + n : count + n + 1], (SUBLANES, LANES))
            wide[r, n] = jnp.where(mirrored, b, a)

    def bond(a, b):
        return jnp.where(a * b > 0.0, (0.5 * STEP) * (a + b), 0.0)

    def setup(r, _):
        here = [wide[r + 1, n] for n in range(count)]
        for p in range(planes):
            for c in range(strip):
                n = p * strip + c
                mine = here[n]
                if c:
                    to_left = here[n - 1]
                else:
                    to_left = jnp.where(sub == 0, 0.0, pltpu.roll(here[n + strip - 1], 1, axis=0))
                    w_col[r, p * (strip + 1)] = bond(mine, to_left)
                if c < strip - 1:
                    to_right = here[n + 1]
                else:
                    to_right = pltpu.roll(here[n - strip + 1], SUBLANES - 1, axis=0)
                    to_right = jnp.where(sub == SUBLANES - 1, pltpu.roll(mine, LANES // 2, axis=1), to_right)
                w_col[r, p * (strip + 1) + c + 1] = bond(mine, to_right)
                below = wide[r + 2, n]
                w_row[r, n] = bond(mine, below)
                around = wide[r, n] + below + to_left + to_right
                if p:
                    around = around + here[n - strip]
                if p < planes - 1:
                    around = around + here[n + strip]
                    w_plane[r, n] = bond(mine, here[n + strip])
                big = (0.5 * STEP) * (6.0 * mine + around) + real
                inv = 1.0 / (big * big + imag * imag)
                scale[r, n] = big * inv
                cross[r, n] = imag * inv

    lax.fori_loop(0, tall + 2, spread, None)
    lax.fori_loop(0, tall, setup, None)


def sweep_kernel(shape, own, above, below, w_row, w_col, w_plane, scale, cross, high, low, out, rhs, first, second, left):
    blocks, own_cols, planes, strip = shape
    rows = own.shape[0]
    tall = rows + 2 * DEEP
    count = planes * strip
    line = 2 * count * SUBLANES
    sub = lax.broadcasted_iota(jnp.int32, (SUBLANES, LANES), 0)

    def at(r, n):
        begin = (r * 2 * count + n) * SUBLANES
        return pl.ds(begin if isinstance(r, int) else pl.multiple_of(begin, SUBLANES), SUBLANES)

    def solve(target, totals, r, m):
        a, b = scale[r, m], cross[r, m]
        target[at(r, 2 * m), :] = a * totals[0] + b * totals[1]
        target[at(r, 2 * m + 1), :] = a * totals[1] - b * totals[0]

    for source, offset in ((above, 0), (own, DEEP), (below, DEEP + rows)):

        def start(r, _, source=source, offset=offset):
            for m in range(count):
                pair = [source[r, 2 * m + k] for k in range(2)]
                for k in range(2):
                    rhs[r + offset, 2 * m + k] = pair[k]
                solve(first, pair, r + offset, m)

        lax.fori_loop(0, source.shape[0], start, None)

    def relax(old, new, r):
        def here(m):
            return [old[at(r, 2 * m + k), :] for k in range(2)]

        for p in range(planes):
            base = p * strip
            before = [pltpu.roll(v, 1, axis=0) for v in here(base + strip - 1)]
            across = [pltpu.roll(v, LANES // 2, axis=1) for v in here(base + strip - 1)]
            after = [pltpu.roll(v, SUBLANES - 1, axis=0) for v in here(base)]
            after = [jnp.where(sub == SUBLANES - 1, x, v) for x, v in zip(across, after)]
            for c in range(strip):
                m = base + c
                flank = p * (strip + 1) + c
                totals = []
                for k in range(2):
                    to_left = here(m - 1)[k] if c else before[k]
                    to_right = here(m + 1)[k] if c < strip - 1 else after[k]
                    total = w_col[r, flank] * to_left + w_col[r, flank + 1] * to_right
                    others = w_row[r, m] * old[at(r + 1, 2 * m + k), :] + w_row[r - 1, m] * old[at(r - 1, 2 * m + k), :]
                    mine = rhs[r, 2 * m + k]
                    if p:
                        mine = mine + w_plane[r, m - strip] * here(m - strip)[k]
                    if p < planes - 1:
                        others = others + w_plane[r, m] * here(m + strip)[k]
                    totals.append(mine + (total + others))
                solve(new, totals, r, m)

    old, new = first, second
    for sweep in range(1, SWEEPS):
        depth = tall - 2 * sweep
        rows_a_turn = next(n for n in (5, 6, 4, 7, 2) if depth % n == 0)

        def step(q, _, old=old, new=new, sweep=sweep, rows_a_turn=rows_a_turn):
            for i in range(rows_a_turn):
                relax(old, new, sweep + rows_a_turn * q + i)

        lax.fori_loop(0, depth // rows_a_turn, step, None)
        old, new = new, old

    cells = planes * rows
    for g in range(own_cols // 4):
        for pair in range(2):
            side, place = divmod(2 * g + pair + WIDE, strip)
            for part in range(2):
                for p in range(planes):
                    begin = DEEP * line + ((p * strip + place) * 2 + part) * SUBLANES + side
                    piece = old[pl.ds(begin, rows, stride=line), :]
                    left[pl.ds(g * cells + p * rows, rows), pl.ds((2 * pair + part) * LANES, LANES)] = piece
    values = dot_split(left[...], high, low)
    for g in range(own_cols // 4):
        parts = [values[g * cells : (g + 1) * cells, tf * LANES : (tf + 1) * LANES] for tf in range(4)]
        turned = jnp.concatenate(parts, axis=0).T
        for c, column in enumerate(column_group(g, own_cols)):
            out[pl.ds(column, blocks, stride=own_cols), :] = turned[c * blocks : (c + 1) * blocks]


def update_kernel(got, state, adjoint, new_state, new_adjoint):
    steps, planes, rows, cols = state.shape
    for tile in range(cols // LANES):
        block = got[pl.ds(tile * LANES, LANES), :].T
        for t in range(steps):
            for f, (old, new) in enumerate(((state, new_state), (adjoint, new_adjoint))):
                for p in range(planes):
                    at = ((t * 2 + f) * planes + p) * rows
                    new[t, p, :, pl.ds(tile * LANES, LANES)] = (
                        old[t, p, :, pl.ds(tile * LANES, LANES)] + block[at : at + rows]
                    )


def call(kernel, outs, scratch, flops, moved, *args, places="", limit=VMEM_LIMIT):
    spaces = {"s": pltpu.SMEM, "h": pltpu.HBM, "v": pltpu.VMEM}
    vmem = pl.BlockSpec(memory_space=pltpu.VMEM)
    return pl.pallas_call(
        kernel,
        out_shape=outs,
        in_specs=[pl.BlockSpec(memory_space=spaces[x]) for x in places.ljust(len(args), "v")],
        out_specs=[vmem] * len(outs) if isinstance(outs, list) else vmem,
        scratch_shapes=scratch,
        compiler_params=pltpu.CompilerParams(vmem_limit_bytes=limit),
        cost_estimate=pl.CostEstimate(flops=flops, bytes_accessed=moved, transcendentals=0),
    )(*args)


def v32(*shape):
    return pltpu.VMEM(shape, jnp.float32)


def f32(*shape):
    return jax.ShapeDtypeStruct(shape, jnp.float32)


def shift(block, axis, distance):
    count = lax.axis_size(axis)
    return lax.ppermute(block, axis, [(i, (i + distance) % count) for i in range(count)])


def body(state, adjoint, source, target, conductivity):
    steps, planes, rows, cols = state.shape
    blocks = lax.axis_size("tm")
    me = lax.axis_index("tm")
    own_cols = cols // blocks
    span = own_cols + 2 * WIDE
    strip = span // (2 * SUBLANES)
    count = planes * strip
    line = 2 * count * SUBLANES
    tall = rows + 2 * DEEP
    tiles = cols // LANES
    tile = (SUBLANES, LANES)

    forward, inverse, shifts = transforms(steps * blocks)
    same = np.eye(4).reshape(4, 2, 2)
    forward = forward.reshape(blocks, steps * 2, 2, LANES // 2)
    forward = np.einsum("itks,chp->tcipkhs", forward, same).reshape(4 * LANES, 4 * LANES)
    inverse = inverse.reshape(2, LANES // 2, blocks, steps * 2)
    inverse = np.einsum("ksit,chp->pkhstci", inverse, same).reshape(4 * LANES, 4 * LANES)
    forward_high, forward_low = split_const(forward)
    inverse_high, inverse_low = split_const(inverse)

    edges = tiles * planes * (2 * steps + 1) + planes * rows
    to_down, to_up, last, first = call(
        functools.partial(pack_kernel, own_cols),
        [f32(edges, LANES), f32(edges, LANES), f32(planes, rows, cols), f32(planes, rows, cols)],
        [v32(*state.shape), v32(*state.shape), v32(*conductivity.shape), pltpu.SemaphoreType.DMA((3,))],
        10**5,
        10**6,
        me.reshape(1), state, adjoint, conductivity,
        places="shhh",
        limit=PACK_VMEM,
    )
    top = shift(to_down, "space", 1)
    bottom = shift(to_up, "space", -1)
    prior = shift(last, "tm", 1)
    later = shift(first, "tm", -1)
    partial = call(
        local_kernel,
        f32(LANES, cols),
        [v32(*state.shape)] * 4 + [v32(*conductivity.shape), pltpu.SemaphoreType.DMA((5,))],
        10**7,
        3 * 10**6,
        state, adjoint, source, target, conductivity,
        places="hhhhh",
        limit=WHOLE_VMEM,
    )
    place = lax.axis_index("space")
    sent = call(
        functools.partial(finish_kernel, (blocks, steps, planes, rows, (0, lax.axis_size("space") - 1))),
        f32(blocks, span, LANES),
        [v32(LANES, cols), v32(cols + 2 * WIDE, LANES)],
        10**7,
        3 * 10**6,
        place.reshape(1), partial, to_down, to_up, prior, later, top, bottom,
        places="s",
    )
    got = lax.all_to_all(sent, "tm", 0, 0, tiled=True).reshape(blocks * span, LANES)
    own, up, down = call(
        functools.partial(forward_kernel, (blocks, span, planes, rows)),
        [f32(rows * line, LANES), f32(DEEP * line, LANES), f32(DEEP * line, LANES)],
        [
            v32(span // 4 * planes * rows, 4 * LANES),
            pltpu.VMEM(forward_high.shape, jnp.bfloat16),
            pltpu.VMEM(forward_low.shape, jnp.bfloat16),
            pltpu.SemaphoreType.DMA((2,)),
        ],
        6 * 10**8,
        4 * 10**6,
        got, forward_high, forward_low,
        places="vhh",
    )
    above = shift(down, "space", 1)
    below = shift(up, "space", -1)

    def unpack(packed, end):
        rim = packed[edges - planes * rows :].reshape(planes, rows, LANES)[..., :span]
        return jnp.where(place == end, 0.0, rim)

    kappa = jnp.concatenate([unpack(top, 0), unpack(to_up, -1), unpack(bottom, lax.axis_size("space") - 1)], axis=1)
    kappa = jnp.stack([kappa[..., : span // 2], kappa[..., : span // 2 - 1 : -1]], axis=2)
    kappa = kappa.reshape(planes, 3 * rows, 2, SUBLANES, strip).transpose(1, 3, 2, 0, 4).reshape(3 * rows, SUBLANES, 2 * count)
    kappa = jnp.pad(kappa, ((0, 0), (0, 0), (0, LANES - 2 * count)))
    weights = call(
        functools.partial(weight_kernel, (planes, strip)),
        [
            f32(tall, count, *tile),
            f32(tall, planes * (strip + 1), *tile),
            f32(tall, count - strip, *tile),
            f32(tall, count, *tile),
            f32(tall, count, *tile),
        ],
        [v32(3 * rows, count, *tile)],
        10**9,
        10**7,
        kappa, np.tile(shifts.reshape(2, 2, -1)[:, :1], (1, 2, 1)).reshape(2, LANES),
    )
    back = call(
        functools.partial(sweep_kernel, (blocks, own_cols, planes, strip)),
        f32(blocks * own_cols, LANES),
        [
            v32(tall, 2 * count, *tile),
            v32(tall * line, LANES),
            v32(tall * line, LANES),
            v32(own_cols // 4 * planes * rows, 4 * LANES),
        ],
        10**9,
        6 * 10**6,
        own.reshape(rows, 2 * count, *tile), above.reshape(DEEP, 2 * count, *tile), below.reshape(DEEP, 2 * count, *tile),
        *weights, inverse_high, inverse_low,
    )
    got_back = lax.all_to_all(back, "tm", 0, 0, tiled=True)
    return tuple(
        call(update_kernel, [f32(*state.shape), f32(*state.shape)], [], 10**6, 2 * 10**6, got_back, state, adjoint)
    )


def solution(mesh):
    split = P("tm", None, "space", None)
    return jax.shard_map(
        body,
        mesh=mesh,
        in_specs=(split, split, split, split, P(None, "space", None)),
        out_specs=(split, split),
        check_vma=False,
    )
```
